32 devices in a mesh: row: 4 (over y, core), col: 8 (over z, x).
Axes of the slice: x: 2, y: 2, z: 4, core: 2. Of those that a mesh axis runs over, the one named last changes fastest.
Arguments:
- positions: float32 [32, 3, 1024], P(None, None, ('row', 'col')), may hold values from -1 to 25, as said below
- charges: float32 [1024], P(('row', 'col')), may hold values from -3 to 3
- atom_types: int32 [1024], P(('row', 'col')), may hold values from 0 to 31
- exclusions: int32 [1024], P('row'), may hold values from 0 to 1073741823, as said below
- type_radius: float32 [32], replicated, may hold values from 1.1 to 2
- type_volume: float32 [32], replicated, may hold values from 0.03 to 0.3
Outputs:
- forces: float32 [32, 3, 1024], P(None, None, ('row', 'col'))
- born_radii: float32 [32, 1024], P(None, ('row', 'col'))
The draws below stay inside these ranges and needn't reach their ends.
Inputs may be any that keep to these rules, and one draw needn't show every extreme that they name: `positions`: within one conformation no two atoms are closer than 0.8. Bit k (k < 15) of exclusions[a] marks the pair a, a + k + 1 and bit 15 + k marks the pair a, a - k - 1; the two marks of one pair agree, and no bit names an atom outside 0 to 1023.
All inputs are finite; a program needn't handle non-finite values.
Results may differ from the reference program's by a relative error of at most 0.0003.
Values sent between devices are 32-bit elements; how exact they have to be, the bound alone decides.
No kernel may reach another device: no remote copies, remote signals or barrier semaphores. Data moves between devices by JAX's collectives and lax.ppermute only.
A program may use at most 64 MiB of HBM per device.

```python
import math
from functools import partial
import jax
import jax.numpy as jnp
from jax import lax

REPLICAS = 32
NTYPES = 32
ATOMS = 1024


def draw_positions(key, part):
    key = jax.random.fold_in(key, 11)
    order_key, jitter_key = jax.random.split(key)
    atom_index = jnp.arange(ATOMS, dtype=jnp.int32)
    placement = jax.random.permutation(order_key, ATOMS // 16).astype(jnp.int32)
    brick = placement[atom_index // 16]
    within = atom_index % 16
    lattice = jnp.stack([within % 4 + 4 * (brick % 4), within // 4 + 4 * (brick // 4 % 4), brick // 16]).astype(jnp.float32) * 1.6
    jitter = 0.4 * jnp.tanh(jax.random.normal(jitter_key, (REPLICAS, 3, ATOMS), jnp.float32))
    return lattice[None] + jitter


def draw_exclusions(key, part):
    key = jax.random.fold_in(key, 23)
    atom_index = jnp.arange(ATOMS, dtype=jnp.int32)
    forward = jax.random.randint(key, (ATOMS,), 0, 32768, dtype=jnp.int32)
    centre = ATOMS // 2
    forward = jnp.where((atom_index >= centre - 15) & (atom_index <= centre), 32767, forward)
    headroom = jnp.clip(ATOMS - 1 - atom_index, 0, 15).astype(jnp.int32)
    forward = jnp.bitwise_and(forward, jnp.left_shift(jnp.ones((ATOMS,), jnp.int32), headroom) - 1)
    backward = jnp.zeros((ATOMS,), jnp.int32)
    for offset in range(15):
        earlier = jnp.concatenate([jnp.zeros((offset + 1,), jnp.int32), forward[:ATOMS - offset - 1]])
        bitflag = jnp.bitwise_and(jnp.right_shift(earlier, offset), 1)
        backward = jnp.bitwise_or(backward, jnp.left_shift(bitflag, 15 + offset))
    return jnp.bitwise_or(forward, backward)


def set_ends(values, stream_key, low, top_value):
    longest = values.shape.index(max(values.shape))
    spots = []
    for shift in (0, 1):
        where = [jax.random.randint(jax.random.fold_in(stream_key, axis), (), 0, length) for axis, length in enumerate(values.shape)]
        where[longest] = (where[longest] + shift) % values.shape[longest]
        spots.append(tuple(where))
    return values.at[spots[0]].set(low).at[spots[1]].set(top_value)


def block_levels(own_key, extent, cuts, low, high):
    gain = 1.0
    for position, blocks in cuts:
        draws = jax.random.uniform(jax.random.fold_in(jax.random.fold_in(own_key, 6), position), (blocks,), jnp.float32, low / len(cuts), high / len(cuts))
        gain = gain * jnp.repeat(jnp.exp(draws), extent[position] // blocks).reshape((-1,) + (1,) * (len(extent) - 1 - position))
    return gain


def bell_draw(own_key, shape, spread, limit, cuts=(), held_as=jnp.bfloat16):
    drawn = spread * jax.random.normal(own_key, shape, jnp.float32)
    if cuts:
        drawn = drawn * block_levels(own_key, shape, cuts, -0.22, 0.18)
    return jnp.clip(drawn, -limit, limit).astype(held_as)


def setup_inputs(seed: int = 0) -> dict:
    arg_keys = jax.random.split(jax.random.key(seed), 7)
    positions = draw_positions(jax.random.fold_in(arg_keys[6], 71), 0)
    charges = bell_draw(arg_keys[1], (ATOMS,), 0.5, 3.0, ((0, 32),), jnp.float32)
    atom_types = set_ends(jax.random.randint(arg_keys[2], (ATOMS,), 0, NTYPES), jax.random.fold_in(arg_keys[2], 1), 0, NTYPES - 1).astype(jnp.int32)
    exclusions = draw_exclusions(jax.random.fold_in(arg_keys[6], 71), 0)
    type_radius = jnp.clip(jnp.exp(jax.random.uniform(arg_keys[4], (NTYPES,), jnp.float32, math.log(1.1), math.log(2.0))), 1.1, 2.0)
    type_volume = jnp.clip(jnp.exp(jax.random.uniform(arg_keys[5], (NTYPES,), jnp.float32, math.log(0.03), math.log(0.3))), 0.03, 0.3)
    return dict(positions=positions, charges=charges, atom_types=atom_types, exclusions=exclusions, type_radius=type_radius, type_volume=type_volume)


SOLVENT_FACTOR = 1.0 - 1.0 / 78.5

def geometry(rowrep, colrep):
    displace = rowrep[0:3, :, :, None] - colrep[0:3, :, None, :]
    distsq = lax.optimization_barrier(jnp.sum(displace * displace, axis=0))
    return (displace, distsq)

def pair_masks(row_ids, col_ids, row_masks):
    shift_gap = col_ids[None, :] - row_ids[:, None]
    paired = shift_gap != 0
    nearby = paired & (jnp.abs(shift_gap) <= 15)
    bitpos = jnp.where(shift_gap > 0, shift_gap - 1, 14 - shift_gap)
    bitpos = jnp.where(nearby, bitpos, 0).astype(jnp.int32)
    bitflag = jnp.bitwise_and(jnp.right_shift(row_masks[:, None], bitpos), 1)
    excluded = nearby & (bitflag == 1)
    weight = jnp.where(paired & jnp.logical_not(excluded), 1.0, 0.0).astype(jnp.float32)
    return (weight, paired)

def coulomb_grad(displace, distsq, rowatom, colatom, weight, paired):
    guarded = jnp.where(paired[None], distsq, 1.0)
    inverse = lax.rsqrt(guarded)
    factor = -(weight * rowatom[0][:, None] * colatom[0][None, :])[None] * inverse * inverse * inverse
    return lax.optimization_barrier(jnp.sum(factor[None] * displace, axis=3))

def descreen_kernel(rowrep, colrep, rowatom, colatom, row_ids, col_ids, row_masks, coul_first):
    displace, distsq = geometry(rowrep, colrep)
    weight, paired = pair_masks(row_ids, col_ids, row_masks)
    denom = distsq + (colatom[2] * colatom[2])[None, None, :]
    inverse = 1.0 / denom
    descreen = jnp.where(paired[None], colatom[1][None, None, :] * inverse * inverse, 0.0)
    pieces = [lax.optimization_barrier(jnp.sum(descreen, axis=2))[None]]
    if coul_first:
        pieces.append(coulomb_grad(displace, distsq, rowatom, colatom, weight, paired))
    return jnp.concatenate(pieces, axis=0)

def born_kernel(rowrep, colrep, rowatom, colatom, row_ids, col_ids, row_masks, coul_last):
    displace, distsq = geometry(rowrep, colrep)
    radius_row = rowrep[3][:, :, None]
    radius_col = colrep[3][:, None, :]
    product = radius_row * radius_col
    damping = jnp.exp(-distsq / (4.0 * product))
    effective = distsq + product * damping
    reciprocal = lax.rsqrt(effective)
    cubed = reciprocal * reciprocal * reciprocal
    charge_pair = SOLVENT_FACTOR * (rowatom[0][:, None] * colatom[0][None, :])[None]
    direct = lax.optimization_barrier(jnp.sum((charge_pair * cubed * (1.0 - 0.25 * damping))[None] * displace, axis=3))
    radial = lax.optimization_barrier(jnp.sum(0.5 * charge_pair * cubed * damping * (1.0 + distsq / (4.0 * product)) * radius_col, axis=2))
    pieces = [radial[None], direct]
    if coul_last:
        weight, paired = pair_masks(row_ids, col_ids, row_masks)
        pieces.append(coulomb_grad(displace, distsq, rowatom, colatom, weight, paired))
    return jnp.concatenate(pieces, axis=0)

def chain_kernel(rowrep, colrep, rowatom, colatom, row_ids, col_ids, row_masks):
    displace, distsq = geometry(rowrep, colrep)
    weight, paired = pair_masks(row_ids, col_ids, row_masks)
    inv_row = 1.0 / (distsq + (rowatom[2] * rowatom[2])[None, :, None])
    inv_col = 1.0 / (distsq + (colatom[2] * colatom[2])[None, None, :])
    factor = rowrep[3][:, :, None] * colatom[1][None, None, :] * inv_col * inv_col * inv_col
    factor = factor + colrep[3][:, None, :] * rowatom[1][None, :, None] * inv_row * inv_row * inv_row
    factor = jnp.where(paired[None], -4.0 * factor, 0.0)
    return lax.optimization_barrier(jnp.sum(factor[None] * displace, axis=3))

def radii(radius, integral):
    saturation = jnp.tanh(radius * integral)
    born = 1.0 / (1.0 / radius - saturation / (radius + 0.09))
    slope = born * born * (1.0 - saturation * saturation) * radius / (radius + 0.09)
    return (born, slope)

def run_pass(kernel, rowrep, colrep, rowatom, colatom, row_ids, col_ids, row_masks, fields):
    planes, replicas, row_len = rowrep.shape
    col_len = colrep.shape[2]
    group = math.gcd(replicas, 8)
    groups = replicas // group
    tile_len = 128 if col_len % 128 == 0 else col_len
    tiles = col_len // tile_len
    row_groups = rowrep.reshape(planes, groups, group, row_len).transpose(1, 0, 2, 3)
    col_groups = colrep.reshape(planes, groups, group, tiles, tile_len).transpose(1, 3, 0, 2, 4)
    col_atoms = colatom.reshape(colatom.shape[0], tiles, tile_len).transpose(1, 0, 2)
    col_tiles = col_ids.reshape(tiles, tile_len)

    def one_group(inputs):
        row_block, col_block = inputs

        def advance(running, pieces):
            col_tile, atom_tile, id_tile = pieces
            return (running + kernel(row_block, col_tile, rowatom, atom_tile, row_ids, id_tile, row_masks), None)
        start = jnp.zeros((fields, group, row_len), jnp.float32)
        running, _ = lax.scan(advance, start, (col_block, col_atoms, col_tiles))
        return running
    result = lax.map(one_group, (row_groups, col_groups))
    return result.transpose(1, 0, 2, 3).reshape(fields, replicas, row_len)

def reference(positions, charges, atom_types, exclusions, type_radius, type_volume):
    count = positions.shape[2]
    radius = type_radius[atom_types]
    volume = type_volume[atom_types]
    atoms = jnp.stack([charges, volume, radius])
    layout = positions.transpose(1, 0, 2)
    atom_ids = jnp.arange(count, dtype=jnp.int32)
    first = run_pass(partial(descreen_kernel, coul_first=False), layout, layout, atoms, atoms, atom_ids, atom_ids, exclusions, 1)
    born, slope = radii(radius[None, :], first[0])
    with_born = jnp.concatenate([layout, born[None]], axis=0)
    second = run_pass(partial(born_kernel, coul_last=True), with_born, with_born, atoms, atoms, atom_ids, atom_ids, exclusions, 7)
    chained = second[0] * slope
    with_chain = jnp.concatenate([layout, chained[None]], axis=0)
    third = run_pass(chain_kernel, with_chain, with_chain, atoms, atoms, atom_ids, atom_ids, exclusions, 3)
    gradient = second[1:4] + second[4:7] + third
    return ((-gradient).transpose(1, 0, 2), born)
```

```python
from functools import partial
import math

import jax
import jax.numpy as jnp
from jax import lax
from jax.experimental import pallas as pl
from jax.experimental.pallas import tpu as pltpu
from jax.sharding import PartitionSpec as P

SOLVENT_FACTOR = 1.0 - 1.0 / 78.5
LANES = 128
SUBLANES = 8
BAND = 15


TURNS = 64
TOGETHER = 21
X, Y, Z, Q, RHO2, VOL, BORN, DECAY, QBORN, CHAIN = range(10)


def pack_kernel(positions_any, charges_any, types_any, marks_any, radius_any, volume_any, out_ref,
                positions, charges, types, marks, radius, volume, arrived):
    moves = []
    for n, (source, target) in enumerate(
        (
            (positions_any, positions),
            (charges_any, charges),
            (types_any, types),
            (marks_any, marks),
            (radius_any, radius),
            (volume_any, volume),
        )
    ):
        moves.append(pltpu.make_async_copy(source, target, arrived.at[n]))
        moves[-1].start()
    for move in moves:
        move.wait()
    replicas, owned = positions.shape[1:]

    def widened(line):
        line = jnp.concatenate([line, jnp.zeros((1, LANES - line.shape[1]), line.dtype)], axis=1)
        return jnp.broadcast_to(line, (SUBLANES, LANES))

    kinds = widened(types[...])

    def look_up(table):
        return jnp.take_along_axis(widened(table[...]), kinds, axis=1, mode="promise_in_bounds")[0:1, :owned]

    per = LANES // owned
    column = lax.axis_index("col")
    forward = jnp.bitwise_and(marks[...], (1 << BAND) - 1).astype(jnp.float32)
    line = lax.broadcasted_iota(jnp.int32, forward.shape, 0)
    picked = jnp.sum(jnp.where(line == lax.div(column, per), forward, 0.0), axis=0, keepdims=True)
    shift = lax.rem(LANES - lax.rem(column, per) * owned, LANES)
    picked = pltpu.roll(jnp.broadcast_to(picked, (SUBLANES, LANES)), shift, 1)[0:1, :owned]

    def everywhere(row):
        return jnp.broadcast_to(row, (replicas, owned))

    first = [positions[0], positions[1], positions[2], everywhere(charges[...])]
    second = [everywhere(look_up(radius)), everywhere(look_up(volume)), everywhere(picked), jnp.zeros((replicas, owned), jnp.float32)]
    out_ref[pl.ds(0, replicas, stride=2), :] = jnp.concatenate(first, axis=1)
    out_ref[pl.ds(1, replicas, stride=2), :] = jnp.concatenate(second, axis=1)


def pack(positions, charges, atom_types, exclusions, type_radius, type_volume):
    replicas, _, owned = positions.shape
    lines = exclusions.shape[0] // LANES
    anywhere = pl.BlockSpec(memory_space=pl.ANY)
    return pl.pallas_call(
        pack_kernel,
        out_shape=jax.ShapeDtypeStruct((replicas * 2, LANES), jnp.float32),
        in_specs=[anywhere] * 6,
        out_specs=pl.BlockSpec(memory_space=pltpu.VMEM),
        scratch_shapes=[
            pltpu.VMEM((3, replicas, owned), jnp.float32),
            pltpu.VMEM((1, owned), jnp.float32),
            pltpu.VMEM((1, owned), jnp.int32),
            pltpu.VMEM((lines, LANES), jnp.int32),
            pltpu.VMEM((1,) + type_radius.shape, jnp.float32),
            pltpu.VMEM((1,) + type_volume.shape, jnp.float32),
            pltpu.SemaphoreType.DMA((6,)),
        ],
        compiler_params=pltpu.CompilerParams(vmem_limit_bytes=60 * 1024 * 1024),
    )(
        positions.transpose(1, 0, 2),
        charges[None],
        atom_types[None],
        exclusions.reshape(lines, LANES),
        type_radius[None],
        type_volume[None],
    )


def conformation_kernel(recv_ref, out_ref, turned, moved, shown, backs, pair_a, pair_b, pair_c, pair_d):
    owners = out_ref.shape[0]
    per = owners // SUBLANES
    owned = LANES // per
    shape = (SUBLANES, LANES)
    half = SUBLANES // 2

    def dense(k):
        part, first = k // per, k % per * owned
        rows = [recv_ref[pl.ds(2 * j + part, SUBLANES, stride=2 * per), :] for j in range(per)]
        return jnp.concatenate([row[:, first : first + owned] for row in rows], axis=1)

    def keep(k, value, move=None):
        for drop in range(SUBLANES):
            turned[k, drop] = pltpu.roll(value, drop, 0) if drop else value
        move = value if move is None else move
        for turn in range(TURNS + 1):
            moved[k, turn] = pltpu.roll(move, turn, 1) if turn else move

    x, y, z, q, rho, vol, marks = [dense(k) for k in range(7)]
    for k, value in ((X, x), (Y, y), (Z, z), (RHO2, rho * rho), (VOL, vol)):
        keep(k, value)
    zero = jnp.zeros(shape, jnp.float32)
    one = jnp.ones(shape, jnp.float32)

    def sweep(pair, names, fields):
        def block(first, turns, drops, stay, two_sided=range(SUBLANES)):
            stayer = {drop: {k: turned[k, drop] for k in names} for drop in drops}
            stay = [list(line) for line in stay]
            for t in range(turns):
                turn = first + t
                mover = {k: moved[k, turn] for k in names}
                back = None
                for n, drop in enumerate(drops):
                    to_mover, to_stayer = pair(mover, stayer[drop], turn, drop)
                    stay[n] = [a + b for a, b in zip(stay[n], to_stayer)]
                    if drop in two_sided:
                        back = to_mover if back is None else [a + b for a, b in zip(back, to_mover)]
                if back is not None:
                    for k in range(fields):
                        backs[k, drops[0] // half, turn] = back[k]
            return stay

        total = [[zero] * 4 for _ in range(fields)]
        for part in range(2):
            drops = list(range(part * half, (part + 1) * half))
            stay = [[zero] * fields for _ in drops]
            for turn in (0, TURNS):
                edge = drops if part == 0 else drops[:1]
                stay[: len(edge)] = block(turn, 1, edge, stay[: len(edge)], two_sided=range(1, half))

            def steps(i, state):
                return block(i * TOGETHER + 1, TOGETHER, drops, state)

            stay = lax.fori_loop(0, (TURNS - 1) // TOGETHER, steps, stay)
            for n, drop in enumerate(drops):
                for k in range(fields):
                    total[k][n] = total[k][n] + (pltpu.roll(stay[n][k], SUBLANES - drop, 0) if drop else stay[n][k])
        for k in range(fields):
            for turn in range(TURNS + 1):
                back = backs[k, 0, turn]
                if turn not in (0, TURNS):
                    back = back + backs[k, 1, turn]
                total[k][turn % 4] = total[k][turn % 4] + (pltpu.roll(back, LANES - turn, 1) if turn else back)
        return [(t[0] + t[1]) + (t[2] + t[3]) for t in total]

    def itself(turn, drop):
        return isinstance(turn, int) and turn == 0 and drop == 0

    def descreen(mover, stayer, turn, drop):
        dx, dy, dz = [mover[k] - stayer[k] for k in (X, Y, Z)]
        distsq = dx * dx + dy * dy + dz * dz
        inv_mover = pltpu.reciprocal(distsq + mover[RHO2], approx=True)
        inv_stayer = pltpu.reciprocal(distsq + stayer[RHO2], approx=True)
        from_mover = mover[VOL] * (inv_mover * inv_mover)
        from_stayer = stayer[VOL] * (inv_stayer * inv_stayer)
        pair_a[turn, drop] = distsq
        pair_b[turn, drop] = from_mover * inv_mover
        pair_c[turn, drop] = from_stayer * inv_stayer
        if itself(turn, drop):
            return [zero], [zero]
        return [from_stayer], [from_mover]

    (integral,) = sweep(descreen, (X, Y, Z, RHO2, VOL), 1)
    saturation = jnp.tanh(rho * integral)
    born = 1.0 / (1.0 / rho - saturation / (rho + 0.09))
    slope = born * born * (1.0 - saturation * saturation) * rho / (rho + 0.09)
    decay = (math.sqrt(math.log2(math.e)) / 2.0) / born
    keep(BORN, born)
    keep(DECAY, decay, -decay)
    keep(QBORN, q * born)

    def born_terms(mover, stayer, turn, drop):
        distsq = pair_a[turn, drop]
        power = distsq * (mover[DECAY] * stayer[DECAY])
        damping = jnp.exp2(power)
        effective = distsq + (mover[BORN] * stayer[BORN]) * damping
        cubed = lax.rsqrt(effective) * pltpu.reciprocal(effective, approx=True)
        pair_d[turn, drop] = cubed * (SOLVENT_FACTOR - (0.25 * SOLVENT_FACTOR) * damping)
        radial = cubed * (damping * (1.0 / math.log(2.0) - power))
        return [radial * stayer[QBORN]], [radial * mover[QBORN]]

    (radial,) = sweep(born_terms, (BORN, DECAY, QBORN), 1)
    chained = (0.5 * SOLVENT_FACTOR * math.log(2.0)) * q * radial * slope
    keep(CHAIN, 4.0 * chained)
    keep(Q, q)
    marks = marks.astype(jnp.int32)
    lane = lax.broadcasted_iota(jnp.int32, shape, 1)
    for turn in range(1, TURNS):
        if turn <= BAND:
            marked = jnp.bitwise_and(jnp.right_shift(pltpu.roll(marks, turn, 1), turn - 1), 1) == 1
            shown[turn, 0] = jnp.where(marked & (lane >= turn), 0.0, 1.0)
            shown[turn, 1] = jnp.where(marked & (lane < turn), 0.0, 1.0)
        else:
            shown[turn, 0] = one
            shown[turn, 1] = one

    def force_terms(mover, stayer, turn, drop):
        if itself(turn, drop):
            return [zero] * 3, [zero] * 3
        distsq = pair_a[turn, drop]
        bare = lax.rsqrt(distsq) * pltpu.reciprocal(distsq, approx=True)
        if drop in (0, SUBLANES - 1) and not isinstance(turn, int):
            bare = bare * shown[turn, min(drop, 1)]
        chain = stayer[CHAIN] * pair_b[turn, drop] + mover[CHAIN] * pair_c[turn, drop]
        factor = chain + (bare - pair_d[turn, drop]) * (mover[Q] * stayer[Q])
        push = [factor * (mover[k] - stayer[k]) for k in (X, Y, Z)]
        return push, [-p for p in push]

    results = sweep(force_terms, (X, Y, Z, Q, CHAIN), 3) + [born]
    for j in range(per):
        out_ref[pl.ds(j, SUBLANES, stride=per), :] = jnp.concatenate(
            [value[:, j * owned : (j + 1) * owned] for value in results], axis=1
        )


def whole_conformation(recv):
    vmem = pl.BlockSpec(memory_space=pltpu.VMEM)
    dense = (SUBLANES, LANES)
    kept = pltpu.VMEM((TURNS + 1, SUBLANES) + dense, jnp.float32)
    return pl.pallas_call(
        conformation_kernel,
        out_shape=jax.ShapeDtypeStruct((recv.shape[0] // 2, LANES), jnp.float32),
        in_specs=[vmem],
        out_specs=vmem,
        scratch_shapes=[
            pltpu.VMEM((10, SUBLANES) + dense, jnp.float32),
            pltpu.VMEM((10, TURNS + 1) + dense, jnp.float32),
            pltpu.VMEM((TURNS, 2) + dense, jnp.float32),
            pltpu.VMEM((3, 2, TURNS + 1) + dense, jnp.float32),
            kept,
            kept,
            kept,
            kept,
        ],
        compiler_params=pltpu.CompilerParams(vmem_limit_bytes=32 * 1024 * 1024),
    )(recv)


def unpack_kernel(back_ref, forces_any, born_any, forces, born, sent):
    owned = born.shape[1]
    born[...] = back_ref[:, 3 * owned : 4 * owned]
    moves = [pltpu.make_async_copy(born, born_any, sent.at[3])]
    moves[0].start()
    for axis in range(3):
        forces[axis] = back_ref[:, axis * owned : (axis + 1) * owned]
        moves.append(pltpu.make_async_copy(forces.at[axis], forces_any.at[axis], sent.at[axis]))
        moves[-1].start()
    for move in moves:
        move.wait()


def unpack(back):
    replicas, width = back.shape
    owned = width // 4
    forces = ((3, replicas, owned), jnp.float32)
    born = ((replicas, owned), jnp.float32)
    anywhere = pl.BlockSpec(memory_space=pl.ANY)
    forces, born = pl.pallas_call(
        unpack_kernel,
        out_shape=[jax.ShapeDtypeStruct(*forces), jax.ShapeDtypeStruct(*born)],
        in_specs=[pl.BlockSpec(memory_space=pltpu.VMEM)],
        out_specs=[anywhere, anywhere],
        scratch_shapes=[pltpu.VMEM(*forces), pltpu.VMEM(*born), pltpu.SemaphoreType.DMA((4,))],
    )(back)
    return (forces.transpose(1, 0, 2), born)


def shared_sum(kernel, own, everyone, fields):
    conformations, planes, count = everyone.shape
    tiles = count // LANES
    tiled = everyone.reshape(conformations, planes, tiles, LANES).transpose(2, 0, 1, 3)
    ids = jnp.arange(count, dtype=jnp.int32).reshape(tiles, LANES)

    def advance(running, piece):
        return (running + kernel(own, *piece), None)

    start = jnp.zeros((fields, conformations, own[0].shape[2]), jnp.float32)
    return lax.scan(advance, start, (tiled, ids))[0]


def split_pair(own, tile):
    atoms = [own[0][:, k, :, None] for k in range(own[0].shape[1])]
    others = [tile[:, k, None, :] for k in range(tile.shape[1])]
    displace = jnp.stack([atoms[k] - others[k] for k in range(3)])
    return (atoms, others, displace, jnp.sum(displace * displace, axis=0))


def shared_descreen(own, tile, ids):
    atoms, others, displace, distsq = split_pair(own, tile)
    inverse = 1.0 / (distsq + others[4] * others[4])
    terms = jnp.where(own[1][:, None] != ids[None, :], others[5] * inverse * inverse, 0.0)
    return jnp.sum(terms, axis=2)[None]


def shared_born(own, tile, ids):
    atoms, others, displace, distsq = split_pair(own, tile)
    gap = ids[None, :] - own[1][:, None]
    nearby = (gap != 0) & (jnp.abs(gap) <= BAND)
    position = jnp.where(nearby, jnp.where(gap > 0, gap - 1, BAND - 1 - gap), 0)
    marked = jnp.bitwise_and(jnp.right_shift(own[2][:, None], position), 1) == 1
    weight = jnp.where((gap == 0) | (nearby & marked), 0.0, 1.0)
    bare = lax.rsqrt(jnp.where(gap == 0, 1.0, distsq))
    product = atoms[6] * others[6]
    power = distsq / (4.0 * product)
    damping = jnp.exp(-power)
    inverse = lax.rsqrt(distsq + product * damping)
    cubed = SOLVENT_FACTOR * (atoms[3] * others[3]) * inverse * inverse * inverse
    radial = jnp.sum(0.5 * cubed * damping * (1.0 + power) * others[6], axis=2)
    coulomb = weight * (atoms[3] * others[3]) * bare * bare * bare
    factor = cubed * (1.0 - 0.25 * damping) - coulomb
    return jnp.concatenate([radial[None], jnp.sum(factor[None] * displace, axis=3)])


def shared_chain(own, tile, ids):
    atoms, others, displace, distsq = split_pair(own, tile)
    inv_own = 1.0 / (distsq + atoms[4] * atoms[4])
    inv_other = 1.0 / (distsq + others[4] * others[4])
    factor = atoms[6] * others[5] * (inv_other * inv_other * inv_other)
    factor = factor + others[6] * atoms[5] * (inv_own * inv_own * inv_own)
    return jnp.sum(-4.0 * factor[None] * displace, axis=3)


def shared_conformation(type_radius, type_volume, packed, exclusions, axis):
    kinds = packed[:, 4].astype(jnp.int32)
    radius = type_radius[kinds]
    volume = type_volume[kinds]
    base = jnp.concatenate([packed[:, :4], radius[:, None], volume[:, None]], axis=1)
    length = packed.shape[2]
    ids = lax.axis_index(axis) * length + jnp.arange(length, dtype=jnp.int32)

    def gathered(block):
        return lax.all_gather(block, axis, axis=2, tiled=True)

    everyone = gathered(base)
    integral = shared_sum(shared_descreen, (base, ids, exclusions), everyone, 1)[0]
    saturation = jnp.tanh(radius * integral)
    born = 1.0 / (1.0 / radius - saturation / (radius + 0.09))
    slope = born * born * (1.0 - saturation * saturation) * radius / (radius + 0.09)
    with_born = jnp.concatenate([everyone, gathered(born[:, None])], axis=1)
    own_born = jnp.concatenate([base, born[:, None]], axis=1)
    second = shared_sum(shared_born, (own_born, ids, exclusions), with_born, 4)
    chained = second[0] * slope
    with_chain = jnp.concatenate([everyone, gathered(chained[:, None])], axis=1)
    own_chain = jnp.concatenate([base, chained[:, None]], axis=1)
    third = shared_sum(shared_chain, (own_chain, ids, exclusions), with_chain, 3)
    return jnp.concatenate([-(second[1:] + third), born[None]]).transpose(1, 0, 2)


def on_device(positions, charges, atom_types, exclusions, type_radius, type_volume):
    replicas, _, owned = positions.shape
    columns = lax.axis_size("col")
    devices = lax.axis_size("row") * columns
    if replicas == devices and devices * owned == SUBLANES * LANES:
        both = ("row", "col")
        packed = pack(positions, charges, atom_types, exclusions, type_radius, type_volume)
        recv = lax.all_to_all(packed.reshape(replicas, 2, LANES), both, split_axis=0, concat_axis=0, tiled=True)
        result = whole_conformation(recv.reshape(replicas * 2, LANES))
        back = lax.all_to_all(result.reshape(replicas, 1, LANES), both, split_axis=0, concat_axis=0, tiled=True)
        return unpack(back.reshape(replicas, LANES))
    shared = jnp.concatenate([charges, atom_types.astype(jnp.float32)])
    planes = [positions.reshape(replicas, 3 * owned), jnp.broadcast_to(shared[None], (replicas, 2 * owned))]
    local = replicas // columns
    recv = lax.all_to_all(jnp.concatenate(planes, axis=1), "col", split_axis=0, concat_axis=0, tiled=True)
    recv = recv.reshape(columns, local, 5, owned).transpose(1, 2, 0, 3).reshape(local, 5, columns * owned)
    result = shared_conformation(type_radius, type_volume, recv, exclusions, "row")
    result = result.reshape(local, 4, columns, owned).transpose(2, 0, 1, 3).reshape(replicas, 4 * owned)
    back = lax.all_to_all(result, "col", split_axis=0, concat_axis=0, tiled=True).reshape(replicas, 4, owned)
    return (back[:, :3], back[:, 3])


def solution(mesh):
    return jax.shard_map(
        on_device,
        mesh=mesh,
        in_specs=(
            P(None, None, ("row", "col")),
            P(("row", "col")),
            P(("row", "col")),
            P("row"),
            P(),
            P(),
        ),
        out_specs=(P(None, None, ("row", "col")), P(None, ("row", "col"))),
        check_vma=False,
    )
```

```python
from functools import partial
import math

import jax
import jax.numpy as jnp
from jax import lax
from jax.experimental import pallas as pl
from jax.experimental.pallas import tpu as pltpu
from jax.sharding import PartitionSpec as P

SOLVENT_FACTOR = 1.0 - 1.0 / 78.5
LANES = 128
SUBLANES = 8
BAND = 15


TURNS = 64
X, Y, Z, Q, RHO2, VOL, BORN, DECAY, QBORN, CHAIN = range(10)


def pack_kernel(positions_any, charges_any, types_any, marks_any, radius_any, volume_any, out_ref,
                positions, charges, types, marks, radius, volume, arrived):
    moves = []
    for n, (source, target) in enumerate(
        (
            (positions_any, positions),
            (charges_any, charges),
            (types_any, types),
            (marks_any, marks),
            (radius_any, radius),
            (volume_any, volume),
        )
    ):
        moves.append(pltpu.make_async_copy(source, target, arrived.at[n]))
        moves[-1].start()
    for move in moves:
        move.wait()
    replicas, owned = positions.shape[1:]

    def widened(line):
        line = jnp.concatenate([line, jnp.zeros((1, LANES - line.shape[1]), line.dtype)], axis=1)
        return jnp.broadcast_to(line, (SUBLANES, LANES))

    kinds = widened(types[...])

    def look_up(table):
        return jnp.take_along_axis(widened(table[...]), kinds, axis=1, mode="promise_in_bounds")[0:1, :owned]

    per = LANES // owned
    column = lax.axis_index("col")
    forward = jnp.bitwise_and(marks[...], (1 << BAND) - 1).astype(jnp.float32)
    line = lax.broadcasted_iota(jnp.int32, forward.shape, 0)
    picked = jnp.sum(jnp.where(line == lax.div(column, per), forward, 0.0), axis=0, keepdims=True)
    shift = lax.rem(LANES - lax.rem(column, per) * owned, LANES)
    picked = pltpu.roll(jnp.broadcast_to(picked, (SUBLANES, LANES)), shift, 1)[0:1, :owned]

    def everywhere(row):
        return jnp.broadcast_to(row, (replicas, owned))

    first = [positions[0], positions[1], positions[2], everywhere(charges[...])]
    second = [everywhere(look_up(radius)), everywhere(look_up(volume)), everywhere(picked), jnp.zeros((replicas, owned), jnp.float32)]
    out_ref[pl.ds(0, replicas, stride=2), :] = jnp.concatenate(first, axis=1)
    out_ref[pl.ds(1, replicas, stride=2), :] = jnp.concatenate(second, axis=1)


def pack(positions, charges, atom_types, exclusions, type_radius, type_volume):
    replicas, _, owned = positions.shape
    lines = exclusions.shape[0] // LANES
    anywhere = pl.BlockSpec(memory_space=pl.ANY)
    return pl.pallas_call(
        pack_kernel,
        out_shape=pltpu.VMEM((replicas * 2, LANES), jnp.float32),
        in_specs=[anywhere] * 6,
        out_specs=pl.BlockSpec(memory_space=pltpu.VMEM),
        scratch_shapes=[
            pltpu.VMEM((3, replicas, owned), jnp.float32),
            pltpu.VMEM((1, owned), jnp.float32),
            pltpu.VMEM((1, owned), jnp.int32),
            pltpu.VMEM((lines, LANES), jnp.int32),
            pltpu.VMEM((1,) + type_radius.shape, jnp.float32),
            pltpu.VMEM((1,) + type_volume.shape, jnp.float32),
            pltpu.SemaphoreType.DMA((6,)),
        ],
        compiler_params=pltpu.CompilerParams(vmem_limit_bytes=4 * 1024 * 1024),
    )(
        *[
            pltpu.with_memory_space_constraint(operand, pltpu.HBM)
            for operand in (
                positions.transpose(1, 0, 2),
                charges[None],
                atom_types[None],
                exclusions.reshape(lines, LANES),
                type_radius[None],
                type_volume[None],
            )
        ]
    )


def conformation_kernel(recv_ref, out_ref, turned, moved, backs, pair_a, pair_b, pair_c, pair_d):
    owners = out_ref.shape[0]
    per = owners // SUBLANES
    owned = LANES // per
    shape = (SUBLANES, LANES)
    half = SUBLANES // 2

    def dense(k):
        part, first = k // per, k % per * owned
        rows = [recv_ref[pl.ds(2 * j + part, SUBLANES, stride=2 * per), :] for j in range(per)]
        return jnp.concatenate([row[:, first : first + owned] for row in rows], axis=1)

    def keep(k, value, move=None):
        for drop in range(SUBLANES):
            turned[k, drop] = pltpu.roll(value, drop, 0) if drop else value
        moved[k, 0] = value if move is None else move

    x, y, z, q, rho, vol, marks = [dense(k) for k in range(7)]
    for k, value in ((X, x), (Y, y), (Z, z), (RHO2, rho * rho), (VOL, vol)):
        keep(k, value)
    zero = jnp.zeros(shape, jnp.float32)
    one = jnp.ones(shape, jnp.float32)

    def sweep(pair, names, fields):
        total = [[zero] * 4 for _ in range(fields)]
        edges = (0, TURNS)
        for part in range(2):
            drops = list(range(part * half, (part + 1) * half))
            stayer = {drop: {k: turned[k, drop] for k in names} for drop in drops}
            stay = {drop: [zero] * fields for drop in drops}
            for turn in range(TURNS + 1):
                if turn == 0:
                    mover = {k: moved[k, 0] for k in names}
                elif part == 0:
                    mover = {k: pltpu.roll(moved[k, 0], turn, 1) for k in names}
                    for k in names:
                        moved[k, turn] = mover[k]
                else:
                    mover = {k: moved[k, turn] for k in names}
                back = None
                for drop in drops:
                    if turn in edges and drop > half:
                        continue
                    to_mover, to_stayer = pair(mover, stayer[drop], turn, drop)
                    stay[drop] = [a + b for a, b in zip(stay[drop], to_stayer)]
                    if turn in edges and drop in (0, half):
                        continue
                    back = to_mover if back is None else [a + b for a, b in zip(back, to_mover)]
                if part == 0 and turn not in edges:
                    for k in range(fields):
                        backs[k, turn] = back[k]
                elif back is not None:
                    for k in range(fields):
                        value = back[k] if turn in edges else back[k] + backs[k, turn]
                        value = pltpu.roll(value, LANES - turn, 1) if turn else value
                        total[k][turn % 4] = total[k][turn % 4] + value
            for n, drop in enumerate(drops):
                for k in range(fields):
                    value = pltpu.roll(stay[drop][k], SUBLANES - drop, 0) if drop else stay[drop][k]
                    total[k][n] = total[k][n] + value
        return [(t[0] + t[1]) + (t[2] + t[3]) for t in total]

    def itself(turn, drop):
        return turn == 0 and drop == 0

    def descreen(mover, stayer, turn, drop):
        dx, dy, dz = [mover[k] - stayer[k] for k in (X, Y, Z)]
        distsq = dx * dx + dy * dy + dz * dz
        inv_mover = pltpu.reciprocal(distsq + mover[RHO2], approx=True)
        inv_stayer = pltpu.reciprocal(distsq + stayer[RHO2], approx=True)
        from_mover = mover[VOL] * (inv_mover * inv_mover)
        from_stayer = stayer[VOL] * (inv_stayer * inv_stayer)
        pair_a[turn, drop] = distsq
        pair_b[turn, drop] = from_mover * inv_mover
        pair_c[turn, drop] = from_stayer * inv_stayer
        if itself(turn, drop):
            return [zero], [zero]
        return [from_stayer], [from_mover]

    (integral,) = sweep(descreen, (X, Y, Z, RHO2, VOL), 1)
    saturation = jnp.tanh(rho * integral)
    born = 1.0 / (1.0 / rho - saturation / (rho + 0.09))
    slope = born * born * (1.0 - saturation * saturation) * rho / (rho + 0.09)
    decay = (math.sqrt(math.log2(math.e)) / 2.0) / born
    keep(BORN, born)
    keep(DECAY, decay, -decay)
    keep(QBORN, q * born)

    def born_terms(mover, stayer, turn, drop):
        distsq = pair_a[turn, drop]
        power = distsq * (mover[DECAY] * stayer[DECAY])
        damping = jnp.exp2(power)
        effective = distsq + (mover[BORN] * stayer[BORN]) * damping
        inverse = lax.rsqrt(effective)
        cubed = inverse * inverse * inverse
        pair_d[turn, drop] = cubed * (SOLVENT_FACTOR - (0.25 * SOLVENT_FACTOR) * damping)
        radial = cubed * (damping * (1.0 / math.log(2.0) - power))
        return [radial * stayer[QBORN]], [radial * mover[QBORN]]

    (radial,) = sweep(born_terms, (BORN, DECAY, QBORN), 1)
    chained = (0.5 * SOLVENT_FACTOR * math.log(2.0)) * q * radial * slope
    keep(CHAIN, 4.0 * chained)
    keep(Q, q)
    marks = marks.astype(jnp.int32)
    lane = lax.broadcasted_iota(jnp.int32, shape, 1)

    def hidden(turn, drop):
        marked = jnp.bitwise_and(jnp.right_shift(pltpu.roll(marks, turn, 1), turn - 1), 1) == 1
        return marked & (lane >= turn if drop == 0 else lane < turn)

    def force_terms(mover, stayer, turn, drop):
        if itself(turn, drop):
            return [zero] * 3, [zero] * 3
        distsq = pair_a[turn, drop]
        bare = lax.rsqrt(distsq)
        bare = bare * bare * bare
        if drop in (0, SUBLANES - 1) and 1 <= turn <= BAND:
            bare = jnp.where(hidden(turn, drop), 0.0, bare)
        chain = stayer[CHAIN] * pair_b[turn, drop] + mover[CHAIN] * pair_c[turn, drop]
        factor = chain + (bare - pair_d[turn, drop]) * (mover[Q] * stayer[Q])
        push = [factor * (mover[k] - stayer[k]) for k in (X, Y, Z)]
        return push, [-p for p in push]

    results = sweep(force_terms, (X, Y, Z, Q, CHAIN), 3) + [born]
    for j in range(per):
        out_ref[pl.ds(j, SUBLANES, stride=per), :] = jnp.concatenate(
            [value[:, j * owned : (j + 1) * owned] for value in results], axis=1
        )


def whole_conformation(recv):
    vmem = pl.BlockSpec(memory_space=pltpu.VMEM)
    dense = (SUBLANES, LANES)
    kept = pltpu.VMEM((TURNS + 1, SUBLANES) + dense, jnp.float32)
    return pl.pallas_call(
        conformation_kernel,
        out_shape=jax.ShapeDtypeStruct((recv.shape[0] // 2, LANES), jnp.float32),
        in_specs=[vmem],
        out_specs=vmem,
        scratch_shapes=[
            pltpu.VMEM((10, SUBLANES) + dense, jnp.float32),
            pltpu.VMEM((10, TURNS + 1) + dense, jnp.float32),
            pltpu.VMEM((3, TURNS + 1) + dense, jnp.float32),
            kept,
            kept,
            kept,
            kept,
        ],
        compiler_params=pltpu.CompilerParams(vmem_limit_bytes=32 * 1024 * 1024),
    )(recv)


def unpack_kernel(back_ref, forces_any, born_any, forces, born, sent):
    owned = born.shape[1]
    born[...] = back_ref[:, 3 * owned : 4 * owned]
    moves = [pltpu.make_async_copy(born, born_any, sent.at[3])]
    moves[0].start()
    for axis in range(3):
        forces[axis] = back_ref[:, axis * owned : (axis + 1) * owned]
        moves.append(pltpu.make_async_copy(forces.at[axis], forces_any.at[axis], sent.at[axis]))
        moves[-1].start()
    for move in moves:
        move.wait()


def unpack(back):
    replicas, width = back.shape
    owned = width // 4
    forces = ((3, replicas, owned), jnp.float32)
    born = ((replicas, owned), jnp.float32)
    anywhere = pl.BlockSpec(memory_space=pl.ANY)
    forces, born = pl.pallas_call(
        unpack_kernel,
        out_shape=[jax.ShapeDtypeStruct(*forces), jax.ShapeDtypeStruct(*born)],
        in_specs=[pl.BlockSpec(memory_space=pltpu.VMEM)],
        out_specs=[anywhere, anywhere],
        scratch_shapes=[pltpu.VMEM(*forces), pltpu.VMEM(*born), pltpu.SemaphoreType.DMA((4,))],
        compiler_params=pltpu.CompilerParams(vmem_limit_bytes=4 * 1024 * 1024),
    )(pltpu.with_memory_space_constraint(back, pltpu.VMEM))
    return (forces.transpose(1, 0, 2), born)


def shared_sum(kernel, own, everyone, fields):
    conformations, planes, count = everyone.shape
    tiles = count // LANES
    tiled = everyone.reshape(conformations, planes, tiles, LANES).transpose(2, 0, 1, 3)
    ids = jnp.arange(count, dtype=jnp.int32).reshape(tiles, LANES)

    def advance(running, piece):
        return (running + kernel(own, *piece), None)

    start = jnp.zeros((fields, conformations, own[0].shape[2]), jnp.float32)
    return lax.scan(advance, start, (tiled, ids))[0]


def split_pair(own, tile):
    atoms = [own[0][:, k, :, None] for k in range(own[0].shape[1])]
    others = [tile[:, k, None, :] for k in range(tile.shape[1])]
    displace = jnp.stack([atoms[k] - others[k] for k in range(3)])
    return (atoms, others, displace, jnp.sum(displace * displace, axis=0))


def shared_descreen(own, tile, ids):
    atoms, others, displace, distsq = split_pair(own, tile)
    inverse = 1.0 / (distsq + others[4] * others[4])
    terms = jnp.where(own[1][:, None] != ids[None, :], others[5] * inverse * inverse, 0.0)
    return jnp.sum(terms, axis=2)[None]


def shared_born(own, tile, ids):
    atoms, others, displace, distsq = split_pair(own, tile)
    gap = ids[None, :] - own[1][:, None]
    nearby = (gap != 0) & (jnp.abs(gap) <= BAND)
    position = jnp.where(nearby, jnp.where(gap > 0, gap - 1, BAND - 1 - gap), 0)
    marked = jnp.bitwise_and(jnp.right_shift(own[2][:, None], position), 1) == 1
    weight = jnp.where((gap == 0) | (nearby & marked), 0.0, 1.0)
    bare = lax.rsqrt(jnp.where(gap == 0, 1.0, distsq))
    product = atoms[6] * others[6]
    power = distsq / (4.0 * product)
    damping = jnp.exp(-power)
    inverse = lax.rsqrt(distsq + product * damping)
    cubed = SOLVENT_FACTOR * (atoms[3] * others[3]) * inverse * inverse * inverse
    radial = jnp.sum(0.5 * cubed * damping * (1.0 + power) * others[6], axis=2)
    coulomb = weight * (atoms[3] * others[3]) * bare * bare * bare
    factor = cubed * (1.0 - 0.25 * damping) - coulomb
    return jnp.concatenate([radial[None], jnp.sum(factor[None] * displace, axis=3)])


def shared_chain(own, tile, ids):
    atoms, others, displace, distsq = split_pair(own, tile)
    inv_own = 1.0 / (distsq + atoms[4] * atoms[4])
    inv_other = 1.0 / (distsq + others[4] * others[4])
    factor = atoms[6] * others[5] * (inv_other * inv_other * inv_other)
    factor = factor + others[6] * atoms[5] * (inv_own * inv_own * inv_own)
    return jnp.sum(-4.0 * factor[None] * displace, axis=3)


def shared_conformation(type_radius, type_volume, packed, exclusions, axis):
    kinds = packed[:, 4].astype(jnp.int32)
    radius = type_radius[kinds]
    volume = type_volume[kinds]
    base = jnp.concatenate([packed[:, :4], radius[:, None], volume[:, None]], axis=1)
    length = packed.shape[2]
    ids = lax.axis_index(axis) * length + jnp.arange(length, dtype=jnp.int32)

    def gathered(block):
        return lax.all_gather(block, axis, axis=2, tiled=True)

    everyone = gathered(base)
    integral = shared_sum(shared_descreen, (base, ids, exclusions), everyone, 1)[0]
    saturation = jnp.tanh(radius * integral)
    born = 1.0 / (1.0 / radius - saturation / (radius + 0.09))
    slope = born * born * (1.0 - saturation * saturation) * radius / (radius + 0.09)
    with_born = jnp.concatenate([everyone, gathered(born[:, None])], axis=1)
    own_born = jnp.concatenate([base, born[:, None]], axis=1)
    second = shared_sum(shared_born, (own_born, ids, exclusions), with_born, 4)
    chained = second[0] * slope
    with_chain = jnp.concatenate([everyone, gathered(chained[:, None])], axis=1)
    own_chain = jnp.concatenate([base, chained[:, None]], axis=1)
    third = shared_sum(shared_chain, (own_chain, ids, exclusions), with_chain, 3)
    return jnp.concatenate([-(second[1:] + third), born[None]]).transpose(1, 0, 2)


def on_device(positions, charges, atom_types, exclusions, type_radius, type_volume):
    replicas, _, owned = positions.shape
    columns = lax.axis_size("col")
    devices = lax.axis_size("row") * columns
    if replicas == devices and devices * owned == SUBLANES * LANES:
        both = ("row", "col")
        packed = pack(positions, charges, atom_types, exclusions, type_radius, type_volume)
        recv = lax.all_to_all(packed.reshape(replicas, 2, LANES), both, split_axis=0, concat_axis=0, tiled=True)
        result = whole_conformation(recv.reshape(replicas * 2, LANES))
        back = lax.all_to_all(result.reshape(replicas, 1, LANES), both, split_axis=0, concat_axis=0, tiled=True)
        return unpack(back.reshape(replicas, LANES))
    shared = jnp.concatenate([charges, atom_types.astype(jnp.float32)])
    planes = [positions.reshape(replicas, 3 * owned), jnp.broadcast_to(shared[None], (replicas, 2 * owned))]
    local = replicas // columns
    recv = lax.all_to_all(jnp.concatenate(planes, axis=1), "col", split_axis=0, concat_axis=0, tiled=True)
    recv = recv.reshape(columns, local, 5, owned).transpose(1, 2, 0, 3).reshape(local, 5, columns * owned)
    result = shared_conformation(type_radius, type_volume, recv, exclusions, "row")
    result = result.reshape(local, 4, columns, owned).transpose(2, 0, 1, 3).reshape(replicas, 4 * owned)
    back = lax.all_to_all(result, "col", split_axis=0, concat_axis=0, tiled=True).reshape(replicas, 4, owned)
    return (back[:, :3], back[:, 3])


def solution(mesh):
    return jax.shard_map(
        on_device,
        mesh=mesh,
        in_specs=(
            P(None, None, ("row", "col")),
            P(("row", "col")),
            P(("row", "col")),
            P("row"),
            P(),
            P(),
        ),
        out_specs=(P(None, None, ("row", "col")), P(None, ("row", "col"))),
        check_vma=False,
    )
```

```python
from functools import partial
import math

import jax
import jax.numpy as jnp
from jax import lax
from jax.experimental import pallas as pl
from jax.experimental.pallas import tpu as pltpu
from jax.sharding import PartitionSpec as P

SOLVENT_FACTOR = 1.0 - 1.0 / 78.5
LANES = 128
SUBLANES = 8
BAND = 15


TURNS = 64
X, Y, Z, Q, RHO2, VOL, BORN, DECAY, QBORN, CHAIN = range(10)


def pack_kernel(positions_any, charges_any, types_any, marks_any, radius_any, volume_any, out_ref,
                positions, charges, types, marks, radius, volume, arrived):
    moves = []
    for n, (source, target) in enumerate(
        (
            (positions_any, positions),
            (charges_any, charges),
            (types_any, types),
            (marks_any, marks),
            (radius_any, radius),
            (volume_any, volume),
        )
    ):
        moves.append(pltpu.make_async_copy(source, target, arrived.at[n]))
        moves[-1].start()
    for move in moves:
        move.wait()
    replicas, owned = positions.shape[1:]

    def widened(line):
        line = jnp.concatenate([line, jnp.zeros((1, LANES - line.shape[1]), line.dtype)], axis=1)
        return jnp.broadcast_to(line, (SUBLANES, LANES))

    kinds = widened(types[...])

    def look_up(table):
        return jnp.take_along_axis(widened(table[...]), kinds, axis=1, mode="promise_in_bounds")[0:1, :owned]

    per = LANES // owned
    column = lax.axis_index("col")
    forward = jnp.bitwise_and(marks[...], (1 << BAND) - 1).astype(jnp.float32)
    line = lax.broadcasted_iota(jnp.int32, forward.shape, 0)
    picked = jnp.sum(jnp.where(line == lax.div(column, per), forward, 0.0), axis=0, keepdims=True)
    shift = lax.rem(LANES - lax.rem(column, per) * owned, LANES)
    picked = pltpu.roll(jnp.broadcast_to(picked, (SUBLANES, LANES)), shift, 1)[0:1, :owned]

    def everywhere(row):
        return jnp.broadcast_to(row, (replicas, owned))

    first = [positions[0], positions[1], positions[2], everywhere(charges[...])]
    second = [everywhere(look_up(radius)), everywhere(look_up(volume)), everywhere(picked), jnp.zeros((replicas, owned), jnp.float32)]
    rows, columns = lax.axis_size("row"), lax.axis_size("col")
    for part, planes in enumerate((first, second)):
        block = jnp.concatenate(planes, axis=1)
        for r in range(rows):
            out_ref[pl.ds(2 * r + part, columns, stride=2 * rows), :] = block[r * columns : (r + 1) * columns]


def pack(positions, charges, atom_types, exclusions, type_radius, type_volume):
    replicas, _, owned = positions.shape
    lines = exclusions.shape[0] // LANES
    anywhere = pl.BlockSpec(memory_space=pl.ANY)
    return pl.pallas_call(
        pack_kernel,
        out_shape=pltpu.VMEM((replicas * 2, LANES), jnp.float32),
        in_specs=[anywhere] * 6,
        out_specs=pl.BlockSpec(memory_space=pltpu.VMEM),
        scratch_shapes=[
            pltpu.VMEM((3, replicas, owned), jnp.float32),
            pltpu.VMEM((1, owned), jnp.float32),
            pltpu.VMEM((1, owned), jnp.int32),
            pltpu.VMEM((lines, LANES), jnp.int32),
            pltpu.VMEM((1,) + type_radius.shape, jnp.float32),
            pltpu.VMEM((1,) + type_volume.shape, jnp.float32),
            pltpu.SemaphoreType.DMA((6,)),
        ],
        compiler_params=pltpu.CompilerParams(vmem_limit_bytes=4 * 1024 * 1024),
    )(
        *[
            pltpu.with_memory_space_constraint(operand, pltpu.HBM)
            for operand in (
                positions.transpose(1, 0, 2),
                charges[None],
                atom_types[None],
                exclusions.reshape(lines, LANES),
                type_radius[None],
                type_volume[None],
            )
        ]
    )


def conformation_kernel(recv_ref, out_ref, staged, turned, moved, backs, pair_a, pair_b, pair_c, pair_d):
    owners = out_ref.shape[0]
    per = owners // SUBLANES
    owned = LANES // per
    shape = (SUBLANES, LANES)
    half = SUBLANES // 2

    rows, columns = lax.axis_size("row"), lax.axis_size("col")
    for part in range(2):
        for r in range(rows):
            staged[part, r * columns : (r + 1) * columns] = recv_ref[pl.ds(2 * r + part, columns, stride=2 * rows), :]

    def dense(k):
        part, first = k // per, k % per * owned
        rows = [staged[part, pl.ds(j, SUBLANES, stride=per), :] for j in range(per)]
        return jnp.concatenate([row[:, first : first + owned] for row in rows], axis=1)

    def keep(k, value, move=None):
        for drop in range(SUBLANES):
            turned[k, drop] = pltpu.roll(value, drop, 0) if drop else value
        moved[k, 0] = value if move is None else move

    x, y, z, q, rho, vol, marks = [dense(k) for k in range(7)]
    for k, value in ((X, x), (Y, y), (Z, z), (RHO2, rho * rho), (VOL, vol)):
        keep(k, value)
    zero = jnp.zeros(shape, jnp.float32)
    one = jnp.ones(shape, jnp.float32)

    def sweep(pair, names, fields):
        total = [[zero] * 4 for _ in range(fields)]
        edges = (0, TURNS)
        for part in range(2):
            drops = list(range(part * half, (part + 1) * half))
            stayer = {drop: {k: turned[k, drop] for k in names} for drop in drops}
            stay = {drop: [zero] * fields for drop in drops}
            for turn in range(TURNS + 1):
                if turn == 0:
                    mover = {k: moved[k, 0] for k in names}
                elif part == 0:
                    mover = {k: pltpu.roll(moved[k, 0], turn, 1) for k in names}
                    for k in names:
                        moved[k, turn] = mover[k]
                else:
                    mover = {k: moved[k, turn] for k in names}
                back = None
                for drop in drops:
                    if turn in edges and drop > half:
                        continue
                    to_mover, to_stayer = pair(mover, stayer[drop], turn, drop)
                    stay[drop] = [a + b for a, b in zip(stay[drop], to_stayer)]
                    if turn in edges and drop in (0, half):
                        continue
                    back = to_mover if back is None else [a + b for a, b in zip(back, to_mover)]
                if part == 0 and turn not in edges:
                    for k in range(fields):
                        backs[k, turn] = back[k]
                elif back is not None:
                    for k in range(fields):
                        value = back[k] if turn in edges else back[k] + backs[k, turn]
                        value = pltpu.roll(value, LANES - turn, 1) if turn else value
                        total[k][turn % 4] = total[k][turn % 4] + value
            for n, drop in enumerate(drops):
                for k in range(fields):
                    value = pltpu.roll(stay[drop][k], SUBLANES - drop, 0) if drop else stay[drop][k]
                    total[k][n] = total[k][n] + value
        return [(t[0] + t[1]) + (t[2] + t[3]) for t in total]

    def itself(turn, drop):
        return turn == 0 and drop == 0

    def descreen(mover, stayer, turn, drop):
        dx, dy, dz = [mover[k] - stayer[k] for k in (X, Y, Z)]
        distsq = dx * dx + dy * dy + dz * dz
        inv_mover = pltpu.reciprocal(distsq + mover[RHO2], approx=True)
        inv_stayer = pltpu.reciprocal(distsq + stayer[RHO2], approx=True)
        from_mover = mover[VOL] * (inv_mover * inv_mover)
        from_stayer = stayer[VOL] * (inv_stayer * inv_stayer)
        pair_a[turn, drop] = distsq
        pair_b[turn, drop] = from_mover * inv_mover
        pair_c[turn, drop] = from_stayer * inv_stayer
        if itself(turn, drop):
            return [zero], [zero]
        return [from_stayer], [from_mover]

    (integral,) = sweep(descreen, (X, Y, Z, RHO2, VOL), 1)
    saturation = jnp.tanh(rho * integral)
    born = 1.0 / (1.0 / rho - saturation / (rho + 0.09))
    slope = born * born * (1.0 - saturation * saturation) * rho / (rho + 0.09)
    decay = (math.sqrt(math.log2(math.e)) / 2.0) / born
    keep(BORN, born)
    keep(DECAY, decay, -decay)
    keep(QBORN, q * born)

    def born_terms(mover, stayer, turn, drop):
        distsq = pair_a[turn, drop]
        power = distsq * (mover[DECAY] * stayer[DECAY])
        damping = jnp.exp2(power)
        effective = distsq + (mover[BORN] * stayer[BORN]) * damping
        inverse = lax.rsqrt(effective)
        cubed = inverse * inverse * inverse
        pair_d[turn, drop] = cubed * (SOLVENT_FACTOR - (0.25 * SOLVENT_FACTOR) * damping)
        radial = cubed * (damping * (1.0 / math.log(2.0) - power))
        return [radial * stayer[QBORN]], [radial * mover[QBORN]]

    (radial,) = sweep(born_terms, (BORN, DECAY, QBORN), 1)
    chained = (0.5 * SOLVENT_FACTOR * math.log(2.0)) * q * radial * slope
    keep(CHAIN, 4.0 * chained)
    keep(Q, q)
    marks = marks.astype(jnp.int32)
    lane = lax.broadcasted_iota(jnp.int32, shape, 1)

    def hidden(turn, drop):
        marked = jnp.bitwise_and(jnp.right_shift(pltpu.roll(marks, turn, 1), turn - 1), 1) == 1
        return marked & (lane >= turn if drop == 0 else lane < turn)

    def force_terms(mover, stayer, turn, drop):
        if itself(turn, drop):
            return [zero] * 3, [zero] * 3
        distsq = pair_a[turn, drop]
        bare = lax.rsqrt(distsq)
        bare = bare * bare * bare
        if drop in (0, SUBLANES - 1) and 1 <= turn <= BAND:
            bare = jnp.where(hidden(turn, drop), 0.0, bare)
        chain = stayer[CHAIN] * pair_b[turn, drop] + mover[CHAIN] * pair_c[turn, drop]
        factor = chain + (bare - pair_d[turn, drop]) * (mover[Q] * stayer[Q])
        push = [factor * (mover[k] - stayer[k]) for k in (X, Y, Z)]
        return push, [-p for p in push]

    results = sweep(force_terms, (X, Y, Z, Q, CHAIN), 3) + [born]
    for j in range(per):
        staged[0, pl.ds(j, SUBLANES, stride=per), :] = jnp.concatenate(
            [value[:, j * owned : (j + 1) * owned] for value in results], axis=1
        )
    for r in range(rows):
        out_ref[pl.ds(r, columns, stride=rows), :] = staged[0, r * columns : (r + 1) * columns]


def whole_conformation(recv):
    vmem = pl.BlockSpec(memory_space=pltpu.VMEM)
    dense = (SUBLANES, LANES)
    kept = pltpu.VMEM((TURNS + 1, SUBLANES) + dense, jnp.float32)
    return pl.pallas_call(
        conformation_kernel,
        out_shape=jax.ShapeDtypeStruct((recv.shape[0] // 2, LANES), jnp.float32),
        in_specs=[vmem],
        out_specs=vmem,
        scratch_shapes=[
            pltpu.VMEM((2, recv.shape[0] // 2, LANES), jnp.float32),
            pltpu.VMEM((10, SUBLANES) + dense, jnp.float32),
            pltpu.VMEM((10, TURNS + 1) + dense, jnp.float32),
            pltpu.VMEM((3, TURNS + 1) + dense, jnp.float32),
            kept,
            kept,
            kept,
            kept,
        ],
        compiler_params=pltpu.CompilerParams(vmem_limit_bytes=32 * 1024 * 1024),
    )(recv)


def unpack_kernel(back_ref, forces_any, born_any, forces, born, sent):
    owned = born.shape[1]
    rows, columns = lax.axis_size("row"), lax.axis_size("col")
    by_row = [back_ref[pl.ds(r, columns, stride=rows), :] for r in range(rows)]

    def lay_out(target, plane):
        for r in range(rows):
            target[r * columns : (r + 1) * columns, :] = by_row[r][:, plane * owned : (plane + 1) * owned]

    lay_out(born, 3)
    moves = [pltpu.make_async_copy(born, born_any, sent.at[3])]
    moves[0].start()
    for axis in range(3):
        lay_out(forces.at[axis], axis)
        moves.append(pltpu.make_async_copy(forces.at[axis], forces_any.at[axis], sent.at[axis]))
        moves[-1].start()
    for move in moves:
        move.wait()


def unpack(back):
    replicas, width = back.shape
    owned = width // 4
    forces = ((3, replicas, owned), jnp.float32)
    born = ((replicas, owned), jnp.float32)
    anywhere = pl.BlockSpec(memory_space=pl.ANY)
    forces, born = pl.pallas_call(
        unpack_kernel,
        out_shape=[jax.ShapeDtypeStruct(*forces), jax.ShapeDtypeStruct(*born)],
        in_specs=[pl.BlockSpec(memory_space=pltpu.VMEM)],
        out_specs=[anywhere, anywhere],
        scratch_shapes=[pltpu.VMEM(*forces), pltpu.VMEM(*born), pltpu.SemaphoreType.DMA((4,))],
        compiler_params=pltpu.CompilerParams(vmem_limit_bytes=4 * 1024 * 1024),
    )(pltpu.with_memory_space_constraint(back, pltpu.VMEM))
    return (forces.transpose(1, 0, 2), born)


def shared_sum(kernel, own, everyone, fields):
    conformations, planes, count = everyone.shape
    tiles = count // LANES
    tiled = everyone.reshape(conformations, planes, tiles, LANES).transpose(2, 0, 1, 3)
    ids = jnp.arange(count, dtype=jnp.int32).reshape(tiles, LANES)

    def advance(running, piece):
        return (running + kernel(own, *piece), None)

    start = jnp.zeros((fields, conformations, own[0].shape[2]), jnp.float32)
    return lax.scan(advance, start, (tiled, ids))[0]


def split_pair(own, tile):
    atoms = [own[0][:, k, :, None] for k in range(own[0].shape[1])]
    others = [tile[:, k, None, :] for k in range(tile.shape[1])]
    displace = jnp.stack([atoms[k] - others[k] for k in range(3)])
    return (atoms, others, displace, jnp.sum(displace * displace, axis=0))


def shared_descreen(own, tile, ids):
    atoms, others, displace, distsq = split_pair(own, tile)
    inverse = 1.0 / (distsq + others[4] * others[4])
    terms = jnp.where(own[1][:, None] != ids[None, :], others[5] * inverse * inverse, 0.0)
    return jnp.sum(terms, axis=2)[None]


def shared_born(own, tile, ids):
    atoms, others, displace, distsq = split_pair(own, tile)
    gap = ids[None, :] - own[1][:, None]
    nearby = (gap != 0) & (jnp.abs(gap) <= BAND)
    position = jnp.where(nearby, jnp.where(gap > 0, gap - 1, BAND - 1 - gap), 0)
    marked = jnp.bitwise_and(jnp.right_shift(own[2][:, None], position), 1) == 1
    weight = jnp.where((gap == 0) | (nearby & marked), 0.0, 1.0)
    bare = lax.rsqrt(jnp.where(gap == 0, 1.0, distsq))
    product = atoms[6] * others[6]
    power = distsq / (4.0 * product)
    damping = jnp.exp(-power)
    inverse = lax.rsqrt(distsq + product * damping)
    cubed = SOLVENT_FACTOR * (atoms[3] * others[3]) * inverse * inverse * inverse
    radial = jnp.sum(0.5 * cubed * damping * (1.0 + power) * others[6], axis=2)
    coulomb = weight * (atoms[3] * others[3]) * bare * bare * bare
    factor = cubed * (1.0 - 0.25 * damping) - coulomb
    return jnp.concatenate([radial[None], jnp.sum(factor[None] * displace, axis=3)])


def shared_chain(own, tile, ids):
    atoms, others, displace, distsq = split_pair(own, tile)
    inv_own = 1.0 / (distsq + atoms[4] * atoms[4])
    inv_other = 1.0 / (distsq + others[4] * others[4])
    factor = atoms[6] * others[5] * (inv_other * inv_other * inv_other)
    factor = factor + others[6] * atoms[5] * (inv_own * inv_own * inv_own)
    return jnp.sum(-4.0 * factor[None] * displace, axis=3)


def shared_conformation(type_radius, type_volume, packed, exclusions, axis):
    kinds = packed[:, 4].astype(jnp.int32)
    radius = type_radius[kinds]
    volume = type_volume[kinds]
    base = jnp.concatenate([packed[:, :4], radius[:, None], volume[:, None]], axis=1)
    length = packed.shape[2]
    ids = lax.axis_index(axis) * length + jnp.arange(length, dtype=jnp.int32)

    def gathered(block):
        return lax.all_gather(block, axis, axis=2, tiled=True)

    everyone = gathered(base)
    integral = shared_sum(shared_descreen, (base, ids, exclusions), everyone, 1)[0]
    saturation = jnp.tanh(radius * integral)
    born = 1.0 / (1.0 / radius - saturation / (radius + 0.09))
    slope = born * born * (1.0 - saturation * saturation) * radius / (radius + 0.09)
    with_born = jnp.concatenate([everyone, gathered(born[:, None])], axis=1)
    own_born = jnp.concatenate([base, born[:, None]], axis=1)
    second = shared_sum(shared_born, (own_born, ids, exclusions), with_born, 4)
    chained = second[0] * slope
    with_chain = jnp.concatenate([everyone, gathered(chained[:, None])], axis=1)
    own_chain = jnp.concatenate([base, chained[:, None]], axis=1)
    third = shared_sum(shared_chain, (own_chain, ids, exclusions), with_chain, 3)
    return jnp.concatenate([-(second[1:] + third), born[None]]).transpose(1, 0, 2)


def on_device(positions, charges, atom_types, exclusions, type_radius, type_volume):
    replicas, _, owned = positions.shape
    columns = lax.axis_size("col")
    devices = lax.axis_size("row") * columns
    if replicas == devices and devices * owned == SUBLANES * LANES:
        both = ("col", "row")
        packed = pack(positions, charges, atom_types, exclusions, type_radius, type_volume)
        recv = lax.all_to_all(packed.reshape(replicas, 2, LANES), both, split_axis=0, concat_axis=0, tiled=True)
        result = whole_conformation(recv.reshape(replicas * 2, LANES))
        back = lax.all_to_all(result.reshape(replicas, 1, LANES), both, split_axis=0, concat_axis=0, tiled=True)
        return unpack(back.reshape(replicas, LANES))
    shared = jnp.concatenate([charges, atom_types.astype(jnp.float32)])
    planes = [positions.reshape(replicas, 3 * owned), jnp.broadcast_to(shared[None], (replicas, 2 * owned))]
    local = replicas // columns
    recv = lax.all_to_all(jnp.concatenate(planes, axis=1), "col", split_axis=0, concat_axis=0, tiled=True)
    recv = recv.reshape(columns, local, 5, owned).transpose(1, 2, 0, 3).reshape(local, 5, columns * owned)
    result = shared_conformation(type_radius, type_volume, recv, exclusions, "row")
    result = result.reshape(local, 4, columns, owned).transpose(2, 0, 1, 3).reshape(replicas, 4 * owned)
    back = lax.all_to_all(result, "col", split_axis=0, concat_axis=0, tiled=True).reshape(replicas, 4, owned)
    return (back[:, :3], back[:, 3])


def solution(mesh):
    return jax.shard_map(
        on_device,
        mesh=mesh,
        in_specs=(
            P(None, None, ("row", "col")),
            P(("row", "col")),
            P(("row", "col")),
            P("row"),
            P(),
            P(),
        ),
        out_specs=(P(None, None, ("row", "col")), P(None, ("row", "col"))),
        check_vma=False,
    )
```

```python
from functools import partial
import math

import jax
import jax.numpy as jnp
from jax import lax
from jax.experimental import pallas as pl
from jax.experimental.pallas import tpu as pltpu
from jax.sharding import PartitionSpec as P

SOLVENT_FACTOR = 1.0 - 1.0 / 78.5
LANES = 128
SUBLANES = 8
BAND = 15


TURNS = 64
X, Y, Z, Q, RHO2, VOL, BORN, DECAY, QBORN, CHAIN = range(10)


def pack_kernel(positions_any, charges_any, types_any, marks_any, radius_any, volume_any, out_ref,
                positions, charges, types, marks, radius, volume, arrived):
    moves = []
    for n, (source, target) in enumerate(
        (
            (positions_any, positions),
            (charges_any, charges),
            (types_any, types),
            (marks_any, marks),
            (radius_any, radius),
            (volume_any, volume),
        )
    ):
        moves.append(pltpu.make_async_copy(source, target, arrived.at[n]))
        moves[-1].start()
    for move in moves:
        move.wait()
    replicas, owned = positions.shape[1:]

    def widened(line):
        line = jnp.concatenate([line, jnp.zeros((1, LANES - line.shape[1]), line.dtype)], axis=1)
        return jnp.broadcast_to(line, (SUBLANES, LANES))

    kinds = widened(types[...])

    def look_up(table):
        return jnp.take_along_axis(widened(table[...]), kinds, axis=1, mode="promise_in_bounds")[0:1, :owned]

    per = LANES // owned
    column = lax.axis_index("col")
    forward = jnp.bitwise_and(marks[...], (1 << BAND) - 1).astype(jnp.float32)
    line = lax.broadcasted_iota(jnp.int32, forward.shape, 0)
    picked = jnp.sum(jnp.where(line == lax.div(column, per), forward, 0.0), axis=0, keepdims=True)
    shift = lax.rem(LANES - lax.rem(column, per) * owned, LANES)
    picked = pltpu.roll(jnp.broadcast_to(picked, (SUBLANES, LANES)), shift, 1)[0:1, :owned]

    def everywhere(row):
        return jnp.broadcast_to(row, (replicas, owned))

    first = [positions[0], positions[1], positions[2], everywhere(charges[...])]
    second = [everywhere(look_up(radius)), everywhere(look_up(volume)), everywhere(picked), jnp.zeros((replicas, owned), jnp.float32)]
    out_ref[pl.ds(0, replicas, stride=2), :] = jnp.concatenate(first, axis=1)
    out_ref[pl.ds(1, replicas, stride=2), :] = jnp.concatenate(second, axis=1)


def pack(positions, charges, atom_types, exclusions, type_radius, type_volume):
    replicas, _, owned = positions.shape
    lines = exclusions.shape[0] // LANES
    anywhere = pl.BlockSpec(memory_space=pl.ANY)
    return pl.pallas_call(
        pack_kernel,
        out_shape=pltpu.VMEM((replicas * 2, LANES), jnp.float32),
        in_specs=[anywhere] * 6,
        out_specs=pl.BlockSpec(memory_space=pltpu.VMEM),
        scratch_shapes=[
            pltpu.VMEM((3, replicas, owned), jnp.float32),
            pltpu.VMEM((1, owned), jnp.float32),
            pltpu.VMEM((1, owned), jnp.int32),
            pltpu.VMEM((lines, LANES), jnp.int32),
            pltpu.VMEM((1,) + type_radius.shape, jnp.float32),
            pltpu.VMEM((1,) + type_volume.shape, jnp.float32),
            pltpu.SemaphoreType.DMA((6,)),
        ],
        compiler_params=pltpu.CompilerParams(vmem_limit_bytes=4 * 1024 * 1024),
    )(
        *[
            pltpu.with_memory_space_constraint(operand, pltpu.HBM)
            for operand in (
                positions.transpose(1, 0, 2),
                charges[None],
                atom_types[None],
                exclusions.reshape(lines, LANES),
                type_radius[None],
                type_volume[None],
            )
        ]
    )


def conformation_kernel(recv_ref, out_ref, turned, moved, backs, pair_a, pair_b, pair_c, pair_d, pair_e):
    owners = out_ref.shape[0]
    per = owners // SUBLANES
    owned = LANES // per
    shape = (SUBLANES, LANES)
    half = SUBLANES // 2

    def dense(k):
        part, first = k // per, k % per * owned
        rows = [recv_ref[pl.ds(2 * j + part, SUBLANES, stride=2 * per), :] for j in range(per)]
        return jnp.concatenate([row[:, first : first + owned] for row in rows], axis=1)

    def keep(k, value, move=None):
        for drop in range(SUBLANES):
            turned[k, drop] = pltpu.roll(value, drop, 0) if drop else value
        moved[k, 0] = value if move is None else move

    x, y, z, q, rho, vol, marks = [dense(k) for k in range(7)]
    for k, value in ((X, x), (Y, y), (Z, z), (RHO2, rho * rho), (VOL, vol)):
        keep(k, value)
    zero = jnp.zeros(shape, jnp.float32)
    one = jnp.ones(shape, jnp.float32)

    def sweep(pair, names, fields):
        total = [[zero] * 4 for _ in range(fields)]
        edges = (0, TURNS)
        for part in range(2):
            drops = list(range(part * half, (part + 1) * half))
            stay = {drop: [zero] * fields for drop in drops}
            for turn in range(TURNS + 1):
                if turn == 0:
                    mover = {k: moved[k, 0] for k in names}
                elif part == 0:
                    for k in names:
                        moved[k, turn] = pltpu.roll(moved[k, 0], turn, 1)
                    mover = {k: moved[k, turn] for k in names}
                else:
                    mover = {k: moved[k, turn] for k in names}
                back = None
                for drop in drops:
                    if turn in edges and drop > half:
                        continue
                    stayer = {k: turned[k, drop] for k in names}
                    to_mover, to_stayer = pair(mover, stayer, turn, drop)
                    stay[drop] = [a + b for a, b in zip(stay[drop], to_stayer)]
                    if turn in edges and drop in (0, half):
                        continue
                    back = to_mover if back is None else [a + b for a, b in zip(back, to_mover)]
                if part == 0 and turn not in edges:
                    for k in range(fields):
                        backs[k, turn] = back[k]
                elif back is not None:
                    for k in range(fields):
                        value = back[k] if turn in edges else back[k] + backs[k, turn]
                        value = pltpu.roll(value, LANES - turn, 1) if turn else value
                        total[k][turn % 4] = total[k][turn % 4] + value
            for n, drop in enumerate(drops):
                for k in range(fields):
                    value = pltpu.roll(stay[drop][k], SUBLANES - drop, 0) if drop else stay[drop][k]
                    total[k][n] = total[k][n] + value
        return [(t[0] + t[1]) + (t[2] + t[3]) for t in total]

    def itself(turn, drop):
        return turn == 0 and drop == 0

    def descreen(mover, stayer, turn, drop):
        dx, dy, dz = [mover[k] - stayer[k] for k in (X, Y, Z)]
        distsq = dx * dx + dy * dy + dz * dz
        inv_mover = pltpu.reciprocal(distsq + mover[RHO2], approx=True)
        inv_stayer = pltpu.reciprocal(distsq + stayer[RHO2], approx=True)
        from_mover = mover[VOL] * (inv_mover * inv_mover)
        from_stayer = stayer[VOL] * (inv_stayer * inv_stayer)
        pair_a[turn, drop] = distsq
        pair_b[turn, drop] = from_mover * inv_mover
        pair_c[turn, drop] = from_stayer * inv_stayer
        if itself(turn, drop):
            return [zero], [zero]
        return [from_stayer], [from_mover]

    (integral,) = sweep(descreen, (X, Y, Z, RHO2, VOL), 1)
    inv_rho = pltpu.reciprocal(rho, approx=True)
    inv_shell = pltpu.reciprocal(rho + 0.09, approx=True)
    saturation = jnp.tanh(rho * integral)
    inv_born = inv_rho - saturation * inv_shell
    born = pltpu.reciprocal(inv_born, approx=True)
    decay = (math.sqrt(math.log2(math.e)) / 2.0) * inv_born
    keep(BORN, born)
    keep(DECAY, decay, -decay)
    keep(QBORN, q * born)
    slope = born * born * (1.0 - saturation * saturation) * (rho * inv_shell)
    to_chain = (2.0 * SOLVENT_FACTOR * math.log(2.0)) * q * slope
    marks = marks.astype(jnp.int32)
    lane = lax.broadcasted_iota(jnp.int32, shape, 1)

    def bare_coulomb(part):
        for turn in range(TURNS + 1):
            if 1 <= turn <= BAND:
                marked = jnp.bitwise_and(jnp.right_shift(pltpu.roll(marks, turn, 1), turn - 1), 1) == 1
            for drop in range(part * half, (part + 1) * half):
                if itself(turn, drop) or (turn in (0, TURNS) and drop > half):
                    continue
                bare = lax.rsqrt(pair_a[turn, drop])
                bare = bare * bare * bare
                if 1 <= turn <= BAND and drop in (0, SUBLANES - 1):
                    bare = jnp.where(marked & (lane >= turn if drop == 0 else lane < turn), 0.0, bare)
                pair_e[turn, drop] = bare

    bare_coulomb(0)

    def born_terms(mover, stayer, turn, drop):
        distsq = pair_a[turn, drop]
        power = distsq * (mover[DECAY] * stayer[DECAY])
        damping = jnp.exp2(power)
        effective = distsq + (mover[BORN] * stayer[BORN]) * damping
        inverse = lax.rsqrt(effective)
        cubed = inverse * inverse * inverse
        pair_d[turn, drop] = cubed * (SOLVENT_FACTOR - (0.25 * SOLVENT_FACTOR) * damping)
        radial = cubed * (damping * (1.0 / math.log(2.0) - power))
        return [radial * stayer[QBORN]], [radial * mover[QBORN]]

    (radial,) = sweep(born_terms, (BORN, DECAY, QBORN), 1)
    keep(CHAIN, radial * to_chain)
    keep(Q, q)
    bare_coulomb(1)

    def force_terms(mover, stayer, turn, drop):
        if itself(turn, drop):
            return [zero] * 3, [zero] * 3
        chain = stayer[CHAIN] * pair_b[turn, drop] + mover[CHAIN] * pair_c[turn, drop]
        factor = chain + (pair_e[turn, drop] - pair_d[turn, drop]) * (mover[Q] * stayer[Q])
        push = [factor * (mover[k] - stayer[k]) for k in (X, Y, Z)]
        return push, [-p for p in push]

    results = sweep(force_terms, (X, Y, Z, Q, CHAIN), 3) + [born]
    for j in range(per):
        out_ref[pl.ds(j, SUBLANES, stride=per), :] = jnp.concatenate(
            [value[:, j * owned : (j + 1) * owned] for value in results], axis=1
        )


def whole_conformation(recv):
    vmem = pl.BlockSpec(memory_space=pltpu.VMEM)
    dense = (SUBLANES, LANES)
    kept = pltpu.VMEM((TURNS + 1, SUBLANES) + dense, jnp.float32)
    return pl.pallas_call(
        conformation_kernel,
        out_shape=jax.ShapeDtypeStruct((recv.shape[0] // 2, LANES), jnp.float32),
        in_specs=[vmem],
        out_specs=vmem,
        scratch_shapes=[
            pltpu.VMEM((10, SUBLANES) + dense, jnp.float32),
            pltpu.VMEM((10, TURNS + 1) + dense, jnp.float32),
            pltpu.VMEM((3, TURNS + 1) + dense, jnp.float32),
            kept,
            kept,
            kept,
            kept,
            kept,
        ],
        compiler_params=pltpu.CompilerParams(vmem_limit_bytes=32 * 1024 * 1024),
    )(recv)


def unpack_kernel(back_ref, forces_any, born_any, forces, born, sent):
    owned = born.shape[1]
    born[...] = back_ref[:, 3 * owned : 4 * owned]
    moves = [pltpu.make_async_copy(born, born_any, sent.at[3])]
    moves[0].start()
    for axis in range(3):
        forces[axis] = back_ref[:, axis * owned : (axis + 1) * owned]
        moves.append(pltpu.make_async_copy(forces.at[axis], forces_any.at[axis], sent.at[axis]))
        moves[-1].start()
    for move in moves:
        move.wait()


def unpack(back):
    replicas, width = back.shape
    owned = width // 4
    forces = ((3, replicas, owned), jnp.float32)
    born = ((replicas, owned), jnp.float32)
    anywhere = pl.BlockSpec(memory_space=pl.ANY)
    forces, born = pl.pallas_call(
        unpack_kernel,
        out_shape=[jax.ShapeDtypeStruct(*forces), jax.ShapeDtypeStruct(*born)],
        in_specs=[pl.BlockSpec(memory_space=pltpu.VMEM)],
        out_specs=[anywhere, anywhere],
        scratch_shapes=[pltpu.VMEM(*forces), pltpu.VMEM(*born), pltpu.SemaphoreType.DMA((4,))],
        compiler_params=pltpu.CompilerParams(vmem_limit_bytes=4 * 1024 * 1024),
    )(pltpu.with_memory_space_constraint(back, pltpu.VMEM))
    return (forces.transpose(1, 0, 2), born)


def shared_sum(kernel, own, everyone, fields):
    conformations, planes, count = everyone.shape
    tiles = count // LANES
    tiled = everyone.reshape(conformations, planes, tiles, LANES).transpose(2, 0, 1, 3)
    ids = jnp.arange(count, dtype=jnp.int32).reshape(tiles, LANES)

    def advance(running, piece):
        return (running + kernel(own, *piece), None)

    start = jnp.zeros((fields, conformations, own[0].shape[2]), jnp.float32)
    return lax.scan(advance, start, (tiled, ids))[0]


def split_pair(own, tile):
    atoms = [own[0][:, k, :, None] for k in range(own[0].shape[1])]
    others = [tile[:, k, None, :] for k in range(tile.shape[1])]
    displace = jnp.stack([atoms[k] - others[k] for k in range(3)])
    return (atoms, others, displace, jnp.sum(displace * displace, axis=0))


def shared_descreen(own, tile, ids):
    atoms, others, displace, distsq = split_pair(own, tile)
    inverse = 1.0 / (distsq + others[4] * others[4])
    terms = jnp.where(own[1][:, None] != ids[None, :], others[5] * inverse * inverse, 0.0)
    return jnp.sum(terms, axis=2)[None]


def shared_born(own, tile, ids):
    atoms, others, displace, distsq = split_pair(own, tile)
    gap = ids[None, :] - own[1][:, None]
    nearby = (gap != 0) & (jnp.abs(gap) <= BAND)
    position = jnp.where(nearby, jnp.where(gap > 0, gap - 1, BAND - 1 - gap), 0)
    marked = jnp.bitwise_and(jnp.right_shift(own[2][:, None], position), 1) == 1
    weight = jnp.where((gap == 0) | (nearby & marked), 0.0, 1.0)
    bare = lax.rsqrt(jnp.where(gap == 0, 1.0, distsq))
    product = atoms[6] * others[6]
    power = distsq / (4.0 * product)
    damping = jnp.exp(-power)
    inverse = lax.rsqrt(distsq + product * damping)
    cubed = SOLVENT_FACTOR * (atoms[3] * others[3]) * inverse * inverse * inverse
    radial = jnp.sum(0.5 * cubed * damping * (1.0 + power) * others[6], axis=2)
    coulomb = weight * (atoms[3] * others[3]) * bare * bare * bare
    factor = cubed * (1.0 - 0.25 * damping) - coulomb
    return jnp.concatenate([radial[None], jnp.sum(factor[None] * displace, axis=3)])


def shared_chain(own, tile, ids):
    atoms, others, displace, distsq = split_pair(own, tile)
    inv_own = 1.0 / (distsq + atoms[4] * atoms[4])
    inv_other = 1.0 / (distsq + others[4] * others[4])
    factor = atoms[6] * others[5] * (inv_other * inv_other * inv_other)
    factor = factor + others[6] * atoms[5] * (inv_own * inv_own * inv_own)
    return jnp.sum(-4.0 * factor[None] * displace, axis=3)


def shared_conformation(type_radius, type_volume, packed, exclusions, axis):
    kinds = packed[:, 4].astype(jnp.int32)
    radius = type_radius[kinds]
    volume = type_volume[kinds]
    base = jnp.concatenate([packed[:, :4], radius[:, None], volume[:, None]], axis=1)
    length = packed.shape[2]
    ids = lax.axis_index(axis) * length + jnp.arange(length, dtype=jnp.int32)

    def gathered(block):
        return lax.all_gather(block, axis, axis=2, tiled=True)

    everyone = gathered(base)
    integral = shared_sum(shared_descreen, (base, ids, exclusions), everyone, 1)[0]
    saturation = jnp.tanh(radius * integral)
    born = 1.0 / (1.0 / radius - saturation / (radius + 0.09))
    slope = born * born * (1.0 - saturation * saturation) * radius / (radius + 0.09)
    with_born = jnp.concatenate([everyone, gathered(born[:, None])], axis=1)
    own_born = jnp.concatenate([base, born[:, None]], axis=1)
    second = shared_sum(shared_born, (own_born, ids, exclusions), with_born, 4)
    chained = second[0] * slope
    with_chain = jnp.concatenate([everyone, gathered(chained[:, None])], axis=1)
    own_chain = jnp.concatenate([base, chained[:, None]], axis=1)
    third = shared_sum(shared_chain, (own_chain, ids, exclusions), with_chain, 3)
    return jnp.concatenate([-(second[1:] + third), born[None]]).transpose(1, 0, 2)


def on_device(positions, charges, atom_types, exclusions, type_radius, type_volume):
    replicas, _, owned = positions.shape
    columns = lax.axis_size("col")
    devices = lax.axis_size("row") * columns
    if replicas == devices and devices * owned == SUBLANES * LANES:
        both = ("row", "col")
        packed = pack(positions, charges, atom_types, exclusions, type_radius, type_volume)
        recv = lax.all_to_all(packed.reshape(replicas, 2, LANES), both, split_axis=0, concat_axis=0, tiled=True)
        result = whole_conformation(recv.reshape(replicas * 2, LANES))
        back = lax.all_to_all(result.reshape(replicas, 1, LANES), both, split_axis=0, concat_axis=0, tiled=True)
        return unpack(back.reshape(replicas, LANES))
    shared = jnp.concatenate([charges, atom_types.astype(jnp.float32)])
    planes = [positions.reshape(replicas, 3 * owned), jnp.broadcast_to(shared[None], (replicas, 2 * owned))]
    local = replicas // columns
    recv = lax.all_to_all(jnp.concatenate(planes, axis=1), "col", split_axis=0, concat_axis=0, tiled=True)
    recv = recv.reshape(columns, local, 5, owned).transpose(1, 2, 0, 3).reshape(local, 5, columns * owned)
    result = shared_conformation(type_radius, type_volume, recv, exclusions, "row")
    result = result.reshape(local, 4, columns, owned).transpose(2, 0, 1, 3).reshape(replicas, 4 * owned)
    back = lax.all_to_all(result, "col", split_axis=0, concat_axis=0, tiled=True).reshape(replicas, 4, owned)
    return (back[:, :3], back[:, 3])


def solution(mesh):
    return jax.shard_map(
        on_device,
        mesh=mesh,
        in_specs=(
            P(None, None, ("row", "col")),
            P(("row", "col")),
            P(("row", "col")),
            P("row"),
            P(),
            P(),
        ),
        out_specs=(P(None, None, ("row", "col")), P(None, ("row", "col"))),
        check_vma=False,
    )
```

```python
from functools import partial
import math

import jax
import jax.numpy as jnp
from jax import lax
from jax.experimental import pallas as pl
from jax.experimental.pallas import tpu as pltpu
from jax.sharding import PartitionSpec as P

SOLVENT_FACTOR = 1.0 - 1.0 / 78.5
LANES = 128
SUBLANES = 8
BAND = 15


TURNS = 64
X, Y, Z, Q, RHO2, VOL, BORN, DECAY, QBORN, CHAIN = range(10)


def pack_kernel(positions_any, charges_any, types_any, marks_any, radius_any, volume_any, out_ref,
                positions, charges, types, marks, radius, volume, arrived):
    moves = []
    for n, (source, target) in enumerate(
        (
            (positions_any, positions),
            (charges_any, charges),
            (types_any, types),
            (marks_any, marks),
            (radius_any, radius),
            (volume_any, volume),
        )
    ):
        moves.append(pltpu.make_async_copy(source, target, arrived.at[n]))
        moves[-1].start()
    for move in moves:
        move.wait()
    replicas, owned = positions.shape[1:]

    def widened(line):
        line = jnp.concatenate([line, jnp.zeros((1, LANES - line.shape[1]), line.dtype)], axis=1)
        return jnp.broadcast_to(line, (SUBLANES, LANES))

    kinds = widened(types[...])

    def look_up(table):
        return jnp.take_along_axis(widened(table[...]), kinds, axis=1, mode="promise_in_bounds")[0:1, :owned]

    per = LANES // owned
    column = lax.axis_index("col")
    forward = jnp.bitwise_and(marks[...], (1 << BAND) - 1).astype(jnp.float32)
    line = lax.broadcasted_iota(jnp.int32, forward.shape, 0)
    picked = jnp.sum(jnp.where(line == lax.div(column, per), forward, 0.0), axis=0, keepdims=True)
    shift = lax.rem(LANES - lax.rem(column, per) * owned, LANES)
    picked = pltpu.roll(jnp.broadcast_to(picked, (SUBLANES, LANES)), shift, 1)[0:1, :owned]

    def everywhere(row):
        return jnp.broadcast_to(row, (replicas, owned))

    first = [positions[0], positions[1], positions[2], everywhere(charges[...])]
    second = [everywhere(look_up(radius)), everywhere(look_up(volume)), everywhere(picked), jnp.zeros((replicas, owned), jnp.float32)]
    out_ref[pl.ds(0, replicas, stride=2), :] = jnp.concatenate(first, axis=1)
    out_ref[pl.ds(1, replicas, stride=2), :] = jnp.concatenate(second, axis=1)


def pack(positions, charges, atom_types, exclusions, type_radius, type_volume):
    replicas, _, owned = positions.shape
    lines = exclusions.shape[0] // LANES
    anywhere = pl.BlockSpec(memory_space=pl.ANY)
    return pl.pallas_call(
        pack_kernel,
        out_shape=pltpu.VMEM((replicas * 2, LANES), jnp.float32),
        in_specs=[anywhere] * 6,
        out_specs=pl.BlockSpec(memory_space=pltpu.VMEM),
        scratch_shapes=[
            pltpu.VMEM((3, replicas, owned), jnp.float32),
            pltpu.VMEM((1, owned), jnp.float32),
            pltpu.VMEM((1, owned), jnp.int32),
            pltpu.VMEM((lines, LANES), jnp.int32),
            pltpu.VMEM((1,) + type_radius.shape, jnp.float32),
            pltpu.VMEM((1,) + type_volume.shape, jnp.float32),
            pltpu.SemaphoreType.DMA((6,)),
        ],
        compiler_params=pltpu.CompilerParams(vmem_limit_bytes=4 * 1024 * 1024),
    )(
        *[
            pltpu.with_memory_space_constraint(operand, pltpu.HBM)
            for operand in (
                positions.transpose(1, 0, 2),
                charges[None],
                atom_types[None],
                exclusions.reshape(lines, LANES),
                type_radius[None],
                type_volume[None],
            )
        ]
    )


def conformation_kernel(recv_ref, out_ref, turned, moved, backs, pair_a, pair_b, pair_c, pair_d, pair_e):
    owners = out_ref.shape[0]
    per = owners // SUBLANES
    owned = LANES // per
    shape = (SUBLANES, LANES)
    half = SUBLANES // 2
    place = lax.axis_index("col")

    def seen(ref, n):
        return ref.at[pl.ds(lax.shift_right_logical(place, 16 + n), ref.shape[0])]

    def dense(k):
        part, first = k // per, k % per * owned
        rows = [recv_ref[pl.ds(2 * j + part, SUBLANES, stride=2 * per), :] for j in range(per)]
        return jnp.concatenate([row[:, first : first + owned] for row in rows], axis=1)

    def keep(k, value, move=None):
        for drop in range(SUBLANES):
            turned[k, drop] = pltpu.roll(value, drop, 0) if drop else value
        moved[k, 0] = value if move is None else move

    x, y, z, q, rho, vol, marks = [dense(k) for k in range(7)]
    for k, value in ((X, x), (Y, y), (Z, z), (RHO2, rho * rho), (VOL, vol)):
        keep(k, value)
    zero = jnp.zeros(shape, jnp.float32)
    one = jnp.ones(shape, jnp.float32)

    def sweep(pair, names, fields):
        total = [[zero] * 4 for _ in range(fields)]
        edges = (0, TURNS)
        moved_later, backs_later = seen(moved, 0), seen(backs, 0)
        for part in range(2):
            drops = list(range(part * half, (part + 1) * half))
            stay = {drop: [zero] * fields for drop in drops}
            for turn in range(TURNS + 1):
                if turn == 0:
                    mover = {k: moved[k, 0] for k in names}
                elif part == 0:
                    mover = {k: pltpu.roll(moved[k, 0], turn, 1) for k in names}
                    for k in names:
                        moved[k, turn] = mover[k]
                else:
                    mover = {k: moved_later[k, turn] for k in names}
                back = None
                for drop in drops:
                    if turn in edges and drop > half:
                        continue
                    stayer = {k: turned[k, drop] for k in names}
                    to_mover, to_stayer = pair(mover, stayer, turn, drop)
                    stay[drop] = [a + b for a, b in zip(stay[drop], to_stayer)]
                    if turn in edges and drop in (0, half):
                        continue
                    back = to_mover if back is None else [a + b for a, b in zip(back, to_mover)]
                if part == 0 and turn not in edges:
                    for k in range(fields):
                        backs[k, turn] = back[k]
                elif back is not None:
                    for k in range(fields):
                        value = back[k] if turn in edges else back[k] + backs_later[k, turn]
                        value = pltpu.roll(value, LANES - turn, 1) if turn else value
                        total[k][turn % 4] = total[k][turn % 4] + value
            for n, drop in enumerate(drops):
                for k in range(fields):
                    value = pltpu.roll(stay[drop][k], SUBLANES - drop, 0) if drop else stay[drop][k]
                    total[k][n] = total[k][n] + value
        return [(t[0] + t[1]) + (t[2] + t[3]) for t in total]

    def itself(turn, drop):
        return turn == 0 and drop == 0

    def descreen(mover, stayer, turn, drop):
        dx, dy, dz = [mover[k] - stayer[k] for k in (X, Y, Z)]
        distsq = dx * dx + dy * dy + dz * dz
        inv_mover = pltpu.reciprocal(distsq + mover[RHO2], approx=True)
        inv_stayer = pltpu.reciprocal(distsq + stayer[RHO2], approx=True)
        from_mover = mover[VOL] * (inv_mover * inv_mover)
        from_stayer = stayer[VOL] * (inv_stayer * inv_stayer)
        pair_a[turn, drop] = distsq
        pair_b[turn, drop] = from_mover * inv_mover
        pair_c[turn, drop] = from_stayer * inv_stayer
        if itself(turn, drop):
            return [zero], [zero]
        return [from_stayer], [from_mover]

    (integral,) = sweep(descreen, (X, Y, Z, RHO2, VOL), 1)
    inv_rho = pltpu.reciprocal(rho, approx=True)
    inv_shell = pltpu.reciprocal(rho + 0.09, approx=True)
    saturation = jnp.tanh(rho * integral)
    inv_born = inv_rho - saturation * inv_shell
    born = pltpu.reciprocal(inv_born, approx=True)
    decay = (math.sqrt(math.log2(math.e)) / 2.0) * inv_born
    keep(BORN, born)
    keep(DECAY, decay, -decay)
    keep(QBORN, q * born)
    slope = born * born * (1.0 - saturation * saturation) * (rho * inv_shell)
    to_chain = (2.0 * SOLVENT_FACTOR * math.log(2.0)) * q * slope
    marks = marks.astype(jnp.int32)
    lane = lax.broadcasted_iota(jnp.int32, shape, 1)

    def bare_coulomb(part):
        distances = seen(pair_a, 1 + part)
        for turn in range(TURNS + 1):
            if 1 <= turn <= BAND:
                marked = jnp.bitwise_and(jnp.right_shift(pltpu.roll(marks, turn, 1), turn - 1), 1) == 1
            for drop in range(part * half, (part + 1) * half):
                if itself(turn, drop) or (turn in (0, TURNS) and drop > half):
                    continue
                bare = lax.rsqrt(distances[turn, drop])
                bare = bare * bare * bare
                if 1 <= turn <= BAND and drop in (0, SUBLANES - 1):
                    bare = jnp.where(marked & (lane >= turn if drop == 0 else lane < turn), 0.0, bare)
                pair_e[turn, drop] = bare

    bare_coulomb(0)

    distances = seen(pair_a, 3)

    def born_terms(mover, stayer, turn, drop):
        distsq = distances[turn, drop]
        power = distsq * (mover[DECAY] * stayer[DECAY])
        damping = jnp.exp2(power)
        effective = distsq + (mover[BORN] * stayer[BORN]) * damping
        inverse = lax.rsqrt(effective)
        cubed = inverse * inverse * inverse
        pair_d[turn, drop] = cubed * (SOLVENT_FACTOR - (0.25 * SOLVENT_FACTOR) * damping)
        radial = cubed * (damping * (1.0 / math.log(2.0) - power))
        return [radial * stayer[QBORN]], [radial * mover[QBORN]]

    (radial,) = sweep(born_terms, (BORN, DECAY, QBORN), 1)
    keep(CHAIN, radial * to_chain)
    keep(Q, q)
    bare_coulomb(1)

    kept_b, kept_c, kept_d, kept_e = [seen(ref, 4) for ref in (pair_b, pair_c, pair_d, pair_e)]

    def force_terms(mover, stayer, turn, drop):
        if itself(turn, drop):
            return [zero] * 3, [zero] * 3
        chain = stayer[CHAIN] * kept_b[turn, drop] + mover[CHAIN] * kept_c[turn, drop]
        factor = chain + (kept_e[turn, drop] - kept_d[turn, drop]) * (mover[Q] * stayer[Q])
        push = [factor * (mover[k] - stayer[k]) for k in (X, Y, Z)]
        return push, [-p for p in push]

    results = sweep(force_terms, (X, Y, Z, Q, CHAIN), 3) + [born]
    for j in range(per):
        out_ref[pl.ds(j, SUBLANES, stride=per), :] = jnp.concatenate(
            [value[:, j * owned : (j + 1) * owned] for value in results], axis=1
        )


def whole_conformation(recv):
    vmem = pl.BlockSpec(memory_space=pltpu.VMEM)
    dense = (SUBLANES, LANES)
    kept = pltpu.VMEM((TURNS + 1, SUBLANES) + dense, jnp.float32)
    return pl.pallas_call(
        conformation_kernel,
        out_shape=jax.ShapeDtypeStruct((recv.shape[0] // 2, LANES), jnp.float32),
        in_specs=[vmem],
        out_specs=vmem,
        scratch_shapes=[
            pltpu.VMEM((10, SUBLANES) + dense, jnp.float32),
            pltpu.VMEM((10, TURNS + 1) + dense, jnp.float32),
            pltpu.VMEM((3, TURNS + 1) + dense, jnp.float32),
            kept,
            kept,
            kept,
            kept,
            kept,
        ],
        compiler_params=pltpu.CompilerParams(vmem_limit_bytes=32 * 1024 * 1024),
    )(recv)


def unpack_kernel(back_ref, forces_any, born_any, forces, born, sent):
    owned = born.shape[1]
    born[...] = back_ref[:, 3 * owned : 4 * owned]
    moves = [pltpu.make_async_copy(born, born_any, sent.at[3])]
    moves[0].start()
    for axis in range(3):
        forces[axis] = back_ref[:, axis * owned : (axis + 1) * owned]
        moves.append(pltpu.make_async_copy(forces.at[axis], forces_any.at[axis], sent.at[axis]))
        moves[-1].start()
    for move in moves:
        move.wait()


def unpack(back):
    replicas, width = back.shape
    owned = width // 4
    forces = ((3, replicas, owned), jnp.float32)
    born = ((replicas, owned), jnp.float32)
    anywhere = pl.BlockSpec(memory_space=pl.ANY)
    forces, born = pl.pallas_call(
        unpack_kernel,
        out_shape=[jax.ShapeDtypeStruct(*forces), jax.ShapeDtypeStruct(*born)],
        in_specs=[pl.BlockSpec(memory_space=pltpu.VMEM)],
        out_specs=[anywhere, anywhere],
        scratch_shapes=[pltpu.VMEM(*forces), pltpu.VMEM(*born), pltpu.SemaphoreType.DMA((4,))],
        compiler_params=pltpu.CompilerParams(vmem_limit_bytes=4 * 1024 * 1024),
    )(pltpu.with_memory_space_constraint(back, pltpu.VMEM))
    return (forces.transpose(1, 0, 2), born)


def shared_sum(kernel, own, everyone, fields):
    conformations, planes, count = everyone.shape
    tiles = count // LANES
    tiled = everyone.reshape(conformations, planes, tiles, LANES).transpose(2, 0, 1, 3)
    ids = jnp.arange(count, dtype=jnp.int32).reshape(tiles, LANES)

    def advance(running, piece):
        return (running + kernel(own, *piece), None)

    start = jnp.zeros((fields, conformations, own[0].shape[2]), jnp.float32)
    return lax.scan(advance, start, (tiled, ids))[0]


def split_pair(own, tile):
    atoms = [own[0][:, k, :, None] for k in range(own[0].shape[1])]
    others = [tile[:, k, None, :] for k in range(tile.shape[1])]
    displace = jnp.stack([atoms[k] - others[k] for k in range(3)])
    return (atoms, others, displace, jnp.sum(displace * displace, axis=0))


def shared_descreen(own, tile, ids):
    atoms, others, displace, distsq = split_pair(own, tile)
    inverse = 1.0 / (distsq + others[4] * others[4])
    terms = jnp.where(own[1][:, None] != ids[None, :], others[5] * inverse * inverse, 0.0)
    return jnp.sum(terms, axis=2)[None]


def shared_born(own, tile, ids):
    atoms, others, displace, distsq = split_pair(own, tile)
    gap = ids[None, :] - own[1][:, None]
    nearby = (gap != 0) & (jnp.abs(gap) <= BAND)
    position = jnp.where(nearby, jnp.where(gap > 0, gap - 1, BAND - 1 - gap), 0)
    marked = jnp.bitwise_and(jnp.right_shift(own[2][:, None], position), 1) == 1
    weight = jnp.where((gap == 0) | (nearby & marked), 0.0, 1.0)
    bare = lax.rsqrt(jnp.where(gap == 0, 1.0, distsq))
    product = atoms[6] * others[6]
    power = distsq / (4.0 * product)
    damping = jnp.exp(-power)
    inverse = lax.rsqrt(distsq + product * damping)
    cubed = SOLVENT_FACTOR * (atoms[3] * others[3]) * inverse * inverse * inverse
    radial = jnp.sum(0.5 * cubed * damping * (1.0 + power) * others[6], axis=2)
    coulomb = weight * (atoms[3] * others[3]) * bare * bare * bare
    factor = cubed * (1.0 - 0.25 * damping) - coulomb
    return jnp.concatenate([radial[None], jnp.sum(factor[None] * displace, axis=3)])


def shared_chain(own, tile, ids):
    atoms, others, displace, distsq = split_pair(own, tile)
    inv_own = 1.0 / (distsq + atoms[4] * atoms[4])
    inv_other = 1.0 / (distsq + others[4] * others[4])
    factor = atoms[6] * others[5] * (inv_other * inv_other * inv_other)
    factor = factor + others[6] * atoms[5] * (inv_own * inv_own * inv_own)
    return jnp.sum(-4.0 * factor[None] * displace, axis=3)


def shared_conformation(type_radius, type_volume, packed, exclusions, axis):
    kinds = packed[:, 4].astype(jnp.int32)
    radius = type_radius[kinds]
    volume = type_volume[kinds]
    base = jnp.concatenate([packed[:, :4], radius[:, None], volume[:, None]], axis=1)
    length = packed.shape[2]
    ids = lax.axis_index(axis) * length + jnp.arange(length, dtype=jnp.int32)

    def gathered(block):
        return lax.all_gather(block, axis, axis=2, tiled=True)

    everyone = gathered(base)
    integral = shared_sum(shared_descreen, (base, ids, exclusions), everyone, 1)[0]
    saturation = jnp.tanh(radius * integral)
    born = 1.0 / (1.0 / radius - saturation / (radius + 0.09))
    slope = born * born * (1.0 - saturation * saturation) * radius / (radius + 0.09)
    with_born = jnp.concatenate([everyone, gathered(born[:, None])], axis=1)
    own_born = jnp.concatenate([base, born[:, None]], axis=1)
    second = shared_sum(shared_born, (own_born, ids, exclusions), with_born, 4)
    chained = second[0] * slope
    with_chain = jnp.concatenate([everyone, gathered(chained[:, None])], axis=1)
    own_chain = jnp.concatenate([base, chained[:, None]], axis=1)
    third = shared_sum(shared_chain, (own_chain, ids, exclusions), with_chain, 3)
    return jnp.concatenate([-(second[1:] + third), born[None]]).transpose(1, 0, 2)


def on_device(positions, charges, atom_types, exclusions, type_radius, type_volume):
    replicas, _, owned = positions.shape
    columns = lax.axis_size("col")
    devices = lax.axis_size("row") * columns
    if replicas == devices and devices * owned == SUBLANES * LANES:
        both = ("row", "col")
        packed = pack(positions, charges, atom_types, exclusions, type_radius, type_volume)
        recv = lax.all_to_all(packed.reshape(replicas, 2, LANES), both, split_axis=0, concat_axis=0, tiled=True)
        result = whole_conformation(recv.reshape(replicas * 2, LANES))
        back = lax.all_to_all(result.reshape(replicas, 1, LANES), both, split_axis=0, concat_axis=0, tiled=True)
        return unpack(back.reshape(replicas, LANES))
    shared = jnp.concatenate([charges, atom_types.astype(jnp.float32)])
    planes = [positions.reshape(replicas, 3 * owned), jnp.broadcast_to(shared[None], (replicas, 2 * owned))]
    local = replicas // columns
    recv = lax.all_to_all(jnp.concatenate(planes, axis=1), "col", split_axis=0, concat_axis=0, tiled=True)
    recv = recv.reshape(columns, local, 5, owned).transpose(1, 2, 0, 3).reshape(local, 5, columns * owned)
    result = shared_conformation(type_radius, type_volume, recv, exclusions, "row")
    result = result.reshape(local, 4, columns, owned).transpose(2, 0, 1, 3).reshape(replicas, 4 * owned)
    back = lax.all_to_all(result, "col", split_axis=0, concat_axis=0, tiled=True).reshape(replicas, 4, owned)
    return (back[:, :3], back[:, 3])


def solution(mesh):
    return jax.shard_map(
        on_device,
        mesh=mesh,
        in_specs=(
            P(None, None, ("row", "col")),
            P(("row", "col")),
            P(("row", "col")),
            P("row"),
            P(),
            P(),
        ),
        out_specs=(P(None, None, ("row", "col")), P(None, ("row", "col"))),
        check_vma=False,
    )
```

```python
from functools import partial
import math

import jax
import jax.numpy as jnp
from jax import lax
from jax.experimental import pallas as pl
from jax.experimental.pallas import tpu as pltpu
from jax.sharding import PartitionSpec as P

SOLVENT_FACTOR = 1.0 - 1.0 / 78.5
LANES = 128
SUBLANES = 8
BAND = 15


TURNS = 64
AHEAD = 5
X, Y, Z, Q, RHO2, VOL, BORN, DECAY, QBORN, CHAIN = range(10)


def pack_kernel(positions_any, charges_any, types_any, marks_any, radius_any, volume_any, out_ref,
                positions, charges, types, marks, radius, volume, arrived):
    moves = []
    for n, (source, target) in enumerate(
        (
            (positions_any, positions),
            (charges_any, charges),
            (types_any, types),
            (marks_any, marks),
            (radius_any, radius),
            (volume_any, volume),
        )
    ):
        moves.append(pltpu.make_async_copy(source, target, arrived.at[n]))
        moves[-1].start()
    for move in moves:
        move.wait()
    replicas, owned = positions.shape[1:]

    def widened(line):
        line = jnp.concatenate([line, jnp.zeros((1, LANES - line.shape[1]), line.dtype)], axis=1)
        return jnp.broadcast_to(line, (SUBLANES, LANES))

    kinds = widened(types[...])

    def look_up(table):
        return jnp.take_along_axis(widened(table[...]), kinds, axis=1, mode="promise_in_bounds")[0:1, :owned]

    per = LANES // owned
    column = lax.axis_index("col")
    forward = jnp.bitwise_and(marks[...], (1 << BAND) - 1).astype(jnp.float32)
    line = lax.broadcasted_iota(jnp.int32, forward.shape, 0)
    picked = jnp.sum(jnp.where(line == lax.div(column, per), forward, 0.0), axis=0, keepdims=True)
    shift = lax.rem(LANES - lax.rem(column, per) * owned, LANES)
    picked = pltpu.roll(jnp.broadcast_to(picked, (SUBLANES, LANES)), shift, 1)[0:1, :owned]

    def everywhere(row):
        return jnp.broadcast_to(row, (replicas, owned))

    first = [positions[0], positions[1], positions[2], everywhere(charges[...])]
    second = [everywhere(look_up(radius)), everywhere(look_up(volume)), everywhere(picked), jnp.zeros((replicas, owned), jnp.float32)]
    out_ref[pl.ds(0, replicas, stride=2), :] = jnp.concatenate(first, axis=1)
    out_ref[pl.ds(1, replicas, stride=2), :] = jnp.concatenate(second, axis=1)


def pack(positions, charges, atom_types, exclusions, type_radius, type_volume):
    replicas, _, owned = positions.shape
    lines = exclusions.shape[0] // LANES
    anywhere = pl.BlockSpec(memory_space=pl.ANY)
    return pl.pallas_call(
        pack_kernel,
        out_shape=pltpu.VMEM((replicas * 2, LANES), jnp.float32),
        in_specs=[anywhere] * 6,
        out_specs=pl.BlockSpec(memory_space=pltpu.VMEM),
        scratch_shapes=[
            pltpu.VMEM((3, replicas, owned), jnp.float32),
            pltpu.VMEM((1, owned), jnp.float32),
            pltpu.VMEM((1, owned), jnp.int32),
            pltpu.VMEM((lines, LANES), jnp.int32),
            pltpu.VMEM((1,) + type_radius.shape, jnp.float32),
            pltpu.VMEM((1,) + type_volume.shape, jnp.float32),
            pltpu.SemaphoreType.DMA((6,)),
        ],
        compiler_params=pltpu.CompilerParams(vmem_limit_bytes=4 * 1024 * 1024),
    )(
        *[
            pltpu.with_memory_space_constraint(operand, pltpu.HBM)
            for operand in (
                positions.transpose(1, 0, 2),
                charges[None],
                atom_types[None],
                exclusions.reshape(lines, LANES),
                type_radius[None],
                type_volume[None],
            )
        ]
    )


def conformation_kernel(recv_ref, out_ref, turned, moved, backs, pair_a, pair_b, pair_c, pair_d, pair_e):
    owners = out_ref.shape[0]
    per = owners // SUBLANES
    owned = LANES // per
    shape = (SUBLANES, LANES)
    half = SUBLANES // 2
    place = lax.axis_index("col")

    def seen(ref, n):
        return ref.at[pl.ds(lax.shift_right_logical(place, 16 + n), ref.shape[0])]

    def dense(k):
        part, first = k // per, k % per * owned
        rows = [recv_ref[pl.ds(2 * j + part, SUBLANES, stride=2 * per), :] for j in range(per)]
        return jnp.concatenate([row[:, first : first + owned] for row in rows], axis=1)

    def keep(k, value, move=None):
        for drop in range(SUBLANES):
            turned[k, drop] = pltpu.roll(value, drop, 0) if drop else value
        moved[k, 0] = value if move is None else move

    x, y, z, q, rho, vol, marks = [dense(k) for k in range(7)]
    for k, value in ((X, x), (Y, y), (Z, z), (RHO2, rho * rho), (VOL, vol)):
        keep(k, value)
    zero = jnp.zeros(shape, jnp.float32)
    one = jnp.ones(shape, jnp.float32)

    def sweep(pair, names, fields):
        total = [[zero] * 4 for _ in range(fields)]
        edges = (0, TURNS)
        moved_later, backs_later = seen(moved, 0), seen(backs, 0)
        for part in range(2):
            drops = list(range(part * half, (part + 1) * half))
            base = {k: moved[k, 0] for k in names}
            stay = {drop: [zero] * fields for drop in drops}
            for turn in range(TURNS + 1):
                if part == 0:
                    for ahead in range(1, AHEAD + 1) if turn == 0 else [turn + AHEAD]:
                        if ahead <= TURNS:
                            for k in names:
                                moved[k, ahead] = pltpu.roll(base[k], ahead, 1)
                mover = {k: moved_later[k, turn] for k in names} if turn else base
                back = None
                for drop in drops:
                    if turn in edges and drop > half:
                        continue
                    stayer = {k: turned[k, drop] for k in names}
                    to_mover, to_stayer = pair(mover, stayer, turn, drop)
                    stay[drop] = [a + b for a, b in zip(stay[drop], to_stayer)]
                    if turn in edges and drop in (0, half):
                        continue
                    back = to_mover if back is None else [a + b for a, b in zip(back, to_mover)]
                if part == 0 and turn not in edges:
                    for k in range(fields):
                        backs[k, turn] = back[k]
                elif back is not None:
                    for k in range(fields):
                        value = back[k] if turn in edges else back[k] + backs_later[k, turn]
                        value = pltpu.roll(value, LANES - turn, 1) if turn else value
                        total[k][turn % 4] = total[k][turn % 4] + value
            for n, drop in enumerate(drops):
                for k in range(fields):
                    value = pltpu.roll(stay[drop][k], SUBLANES - drop, 0) if drop else stay[drop][k]
                    total[k][n] = total[k][n] + value
        return [(t[0] + t[1]) + (t[2] + t[3]) for t in total]

    def itself(turn, drop):
        return turn == 0 and drop == 0

    def descreen(mover, stayer, turn, drop):
        dx, dy, dz = [mover[k] - stayer[k] for k in (X, Y, Z)]
        distsq = dx * dx + dy * dy + dz * dz
        inv_mover = pltpu.reciprocal(distsq + mover[RHO2], approx=True)
        inv_stayer = pltpu.reciprocal(distsq + stayer[RHO2], approx=True)
        from_mover = mover[VOL] * (inv_mover * inv_mover)
        from_stayer = stayer[VOL] * (inv_stayer * inv_stayer)
        pair_a[turn, drop] = distsq
        pair_b[turn, drop] = from_mover * inv_mover
        pair_c[turn, drop] = from_stayer * inv_stayer
        if itself(turn, drop):
            return [zero], [zero]
        return [from_stayer], [from_mover]

    (integral,) = sweep(descreen, (X, Y, Z, RHO2, VOL), 1)
    inv_rho = pltpu.reciprocal(rho, approx=True)
    inv_shell = pltpu.reciprocal(rho + 0.09, approx=True)
    saturation = jnp.tanh(rho * integral)
    inv_born = inv_rho - saturation * inv_shell
    born = pltpu.reciprocal(inv_born, approx=True)
    decay = (math.sqrt(math.log2(math.e)) / 2.0) * inv_born
    keep(BORN, born)
    keep(DECAY, decay, -decay)
    keep(QBORN, q * born)
    slope = born * born * (1.0 - saturation * saturation) * (rho * inv_shell)
    to_chain = (2.0 * SOLVENT_FACTOR * math.log(2.0)) * q * slope
    marks = marks.astype(jnp.int32)
    lane = lax.broadcasted_iota(jnp.int32, shape, 1)

    def bare_coulomb(part):
        distances = seen(pair_a, 1 + part)
        for turn in range(TURNS + 1):
            if 1 <= turn <= BAND:
                marked = jnp.bitwise_and(jnp.right_shift(pltpu.roll(marks, turn, 1), turn - 1), 1) == 1
            for drop in range(part * half, (part + 1) * half):
                if itself(turn, drop) or (turn in (0, TURNS) and drop > half):
                    continue
                bare = lax.rsqrt(distances[turn, drop])
                bare = bare * bare * bare
                if 1 <= turn <= BAND and drop in (0, SUBLANES - 1):
                    bare = jnp.where(marked & (lane >= turn if drop == 0 else lane < turn), 0.0, bare)
                pair_e[turn, drop] = bare

    bare_coulomb(0)

    distances = seen(pair_a, 3)

    def born_terms(mover, stayer, turn, drop):
        distsq = distances[turn, drop]
        power = distsq * (mover[DECAY] * stayer[DECAY])
        damping = jnp.exp2(power)
        effective = distsq + (mover[BORN] * stayer[BORN]) * damping
        inverse = lax.rsqrt(effective)
        cubed = inverse * inverse * inverse
        pair_d[turn, drop] = cubed * (SOLVENT_FACTOR - (0.25 * SOLVENT_FACTOR) * damping)
        radial = cubed * (damping * (1.0 / math.log(2.0) - power))
        return [radial * stayer[QBORN]], [radial * mover[QBORN]]

    (radial,) = sweep(born_terms, (BORN, DECAY, QBORN), 1)
    keep(CHAIN, radial * to_chain)
    keep(Q, q)
    bare_coulomb(1)

    kept_b, kept_c, kept_d, kept_e = [seen(ref, 4) for ref in (pair_b, pair_c, pair_d, pair_e)]

    def force_terms(mover, stayer, turn, drop):
        if itself(turn, drop):
            return [zero] * 3, [zero] * 3
        chain = stayer[CHAIN] * kept_b[turn, drop] + mover[CHAIN] * kept_c[turn, drop]
        factor = chain + (kept_e[turn, drop] - kept_d[turn, drop]) * (mover[Q] * stayer[Q])
        push = [factor * (mover[k] - stayer[k]) for k in (X, Y, Z)]
        return push, [-p for p in push]

    results = sweep(force_terms, (X, Y, Z, Q, CHAIN), 3) + [born]
    for j in range(per):
        out_ref[pl.ds(j, SUBLANES, stride=per), :] = jnp.concatenate(
            [value[:, j * owned : (j + 1) * owned] for value in results], axis=1
        )


def whole_conformation(recv):
    vmem = pl.BlockSpec(memory_space=pltpu.VMEM)
    dense = (SUBLANES, LANES)
    kept = pltpu.VMEM((TURNS + 1, SUBLANES) + dense, jnp.float32)
    return pl.pallas_call(
        conformation_kernel,
        out_shape=jax.ShapeDtypeStruct((recv.shape[0] // 2, LANES), jnp.float32),
        in_specs=[vmem],
        out_specs=vmem,
        scratch_shapes=[
            pltpu.VMEM((10, SUBLANES) + dense, jnp.float32),
            pltpu.VMEM((10, TURNS + 1) + dense, jnp.float32),
            pltpu.VMEM((3, TURNS + 1) + dense, jnp.float32),
            kept,
            kept,
            kept,
            kept,
            kept,
        ],
        compiler_params=pltpu.CompilerParams(vmem_limit_bytes=32 * 1024 * 1024),
    )(recv)


def unpack_kernel(back_ref, forces_any, born_any, forces, born, sent):
    owned = born.shape[1]
    born[...] = back_ref[:, 3 * owned : 4 * owned]
    moves = [pltpu.make_async_copy(born, born_any, sent.at[3])]
    moves[0].start()
    for axis in range(3):
        forces[axis] = back_ref[:, axis * owned : (axis + 1) * owned]
        moves.append(pltpu.make_async_copy(forces.at[axis], forces_any.at[axis], sent.at[axis]))
        moves[-1].start()
    for move in moves:
        move.wait()


def unpack(back):
    replicas, width = back.shape
    owned = width // 4
    forces = ((3, replicas, owned), jnp.float32)
    born = ((replicas, owned), jnp.float32)
    anywhere = pl.BlockSpec(memory_space=pl.ANY)
    forces, born = pl.pallas_call(
        unpack_kernel,
        out_shape=[jax.ShapeDtypeStruct(*forces), jax.ShapeDtypeStruct(*born)],
        in_specs=[pl.BlockSpec(memory_space=pltpu.VMEM)],
        out_specs=[anywhere, anywhere],
        scratch_shapes=[pltpu.VMEM(*forces), pltpu.VMEM(*born), pltpu.SemaphoreType.DMA((4,))],
        compiler_params=pltpu.CompilerParams(vmem_limit_bytes=4 * 1024 * 1024),
    )(pltpu.with_memory_space_constraint(back, pltpu.VMEM))
    return (forces.transpose(1, 0, 2), born)


def shared_sum(kernel, own, everyone, fields):
    conformations, planes, count = everyone.shape
    tiles = count // LANES
    tiled = everyone.reshape(conformations, planes, tiles, LANES).transpose(2, 0, 1, 3)
    ids = jnp.arange(count, dtype=jnp.int32).reshape(tiles, LANES)

    def advance(running, piece):
        return (running + kernel(own, *piece), None)

    start = jnp.zeros((fields, conformations, own[0].shape[2]), jnp.float32)
    return lax.scan(advance, start, (tiled, ids))[0]


def split_pair(own, tile):
    atoms = [own[0][:, k, :, None] for k in range(own[0].shape[1])]
    others = [tile[:, k, None, :] for k in range(tile.shape[1])]
    displace = jnp.stack([atoms[k] - others[k] for k in range(3)])
    return (atoms, others, displace, jnp.sum(displace * displace, axis=0))


def shared_descreen(own, tile, ids):
    atoms, others, displace, distsq = split_pair(own, tile)
    inverse = 1.0 / (distsq + others[4] * others[4])
    terms = jnp.where(own[1][:, None] != ids[None, :], others[5] * inverse * inverse, 0.0)
    return jnp.sum(terms, axis=2)[None]


def shared_born(own, tile, ids):
    atoms, others, displace, distsq = split_pair(own, tile)
    gap = ids[None, :] - own[1][:, None]
    nearby = (gap != 0) & (jnp.abs(gap) <= BAND)
    position = jnp.where(nearby, jnp.where(gap > 0, gap - 1, BAND - 1 - gap), 0)
    marked = jnp.bitwise_and(jnp.right_shift(own[2][:, None], position), 1) == 1
    weight = jnp.where((gap == 0) | (nearby & marked), 0.0, 1.0)
    bare = lax.rsqrt(jnp.where(gap == 0, 1.0, distsq))
    product = atoms[6] * others[6]
    power = distsq / (4.0 * product)
    damping = jnp.exp(-power)
    inverse = lax.rsqrt(distsq + product * damping)
    cubed = SOLVENT_FACTOR * (atoms[3] * others[3]) * inverse * inverse * inverse
    radial = jnp.sum(0.5 * cubed * damping * (1.0 + power) * others[6], axis=2)
    coulomb = weight * (atoms[3] * others[3]) * bare * bare * bare
    factor = cubed * (1.0 - 0.25 * damping) - coulomb
    return jnp.concatenate([radial[None], jnp.sum(factor[None] * displace, axis=3)])


def shared_chain(own, tile, ids):
    atoms, others, displace, distsq = split_pair(own, tile)
    inv_own = 1.0 / (distsq + atoms[4] * atoms[4])
    inv_other = 1.0 / (distsq + others[4] * others[4])
    factor = atoms[6] * others[5] * (inv_other * inv_other * inv_other)
    factor = factor + others[6] * atoms[5] * (inv_own * inv_own * inv_own)
    return jnp.sum(-4.0 * factor[None] * displace, axis=3)


def shared_conformation(type_radius, type_volume, packed, exclusions, axis):
    kinds = packed[:, 4].astype(jnp.int32)
    radius = type_radius[kinds]
    volume = type_volume[kinds]
    base = jnp.concatenate([packed[:, :4], radius[:, None], volume[:, None]], axis=1)
    length = packed.shape[2]
    ids = lax.axis_index(axis) * length + jnp.arange(length, dtype=jnp.int32)

    def gathered(block):
        return lax.all_gather(block, axis, axis=2, tiled=True)

    everyone = gathered(base)
    integral = shared_sum(shared_descreen, (base, ids, exclusions), everyone, 1)[0]
    saturation = jnp.tanh(radius * integral)
    born = 1.0 / (1.0 / radius - saturation / (radius + 0.09))
    slope = born * born * (1.0 - saturation * saturation) * radius / (radius + 0.09)
    with_born = jnp.concatenate([everyone, gathered(born[:, None])], axis=1)
    own_born = jnp.concatenate([base, born[:, None]], axis=1)
    second = shared_sum(shared_born, (own_born, ids, exclusions), with_born, 4)
    chained = second[0] * slope
    with_chain = jnp.concatenate([everyone, gathered(chained[:, None])], axis=1)
    own_chain = jnp.concatenate([base, chained[:, None]], axis=1)
    third = shared_sum(shared_chain, (own_chain, ids, exclusions), with_chain, 3)
    return jnp.concatenate([-(second[1:] + third), born[None]]).transpose(1, 0, 2)


def on_device(positions, charges, atom_types, exclusions, type_radius, type_volume):
    replicas, _, owned = positions.shape
    columns = lax.axis_size("col")
    devices = lax.axis_size("row") * columns
    if replicas == devices and devices * owned == SUBLANES * LANES:
        both = ("row", "col")
        packed = pack(positions, charges, atom_types, exclusions, type_radius, type_volume)
        recv = lax.all_to_all(packed.reshape(replicas, 2, LANES), both, split_axis=0, concat_axis=0, tiled=True)
        result = whole_conformation(recv.reshape(replicas * 2, LANES))
        back = lax.all_to_all(result.reshape(replicas, 1, LANES), both, split_axis=0, concat_axis=0, tiled=True)
        return unpack(back.reshape(replicas, LANES))
    shared = jnp.concatenate([charges, atom_types.astype(jnp.float32)])
    planes = [positions.reshape(replicas, 3 * owned), jnp.broadcast_to(shared[None], (replicas, 2 * owned))]
    local = replicas // columns
    recv = lax.all_to_all(jnp.concatenate(planes, axis=1), "col", split_axis=0, concat_axis=0, tiled=True)
    recv = recv.reshape(columns, local, 5, owned).transpose(1, 2, 0, 3).reshape(local, 5, columns * owned)
    result = shared_conformation(type_radius, type_volume, recv, exclusions, "row")
    result = result.reshape(local, 4, columns, owned).transpose(2, 0, 1, 3).reshape(replicas, 4 * owned)
    back = lax.all_to_all(result, "col", split_axis=0, concat_axis=0, tiled=True).reshape(replicas, 4, owned)
    return (back[:, :3], back[:, 3])


def solution(mesh):
    return jax.shard_map(
        on_device,
        mesh=mesh,
        in_specs=(
            P(None, None, ("row", "col")),
            P(("row", "col")),
            P(("row", "col")),
            P("row"),
            P(),
            P(),
        ),
        out_specs=(P(None, None, ("row", "col")), P(None, ("row", "col"))),
        check_vma=False,
    )
```

```python
from functools import partial
import math

import jax
import jax.numpy as jnp
from jax import lax
from jax.experimental import pallas as pl
from jax.experimental.pallas import tpu as pltpu
from jax.sharding import PartitionSpec as P

SOLVENT_FACTOR = 1.0 - 1.0 / 78.5
LANES = 128
SUBLANES = 8
BAND = 15


TURNS = 64
X, Y, Z, Q, RHO2, VOL, BORN, DECAY, QBORN, CHAIN = range(10)


def pack_kernel(positions_any, charges_any, types_any, marks_any, radius_any, volume_any, out_ref,
                positions, charges, types, marks, radius, volume, arrived):
    moves = []
    for n, (source, target) in enumerate(
        (
            (positions_any, positions),
            (charges_any, charges),
            (types_any, types),
            (marks_any, marks),
            (radius_any, radius),
            (volume_any, volume),
        )
    ):
        moves.append(pltpu.make_async_copy(source, target, arrived.at[n]))
        moves[-1].start()
    for move in moves[1:]:
        move.wait()
    replicas, owned = positions.shape[1:]

    def widened(line):
        line = jnp.concatenate([line, jnp.zeros((1, LANES - line.shape[1]), line.dtype)], axis=1)
        return jnp.broadcast_to(line, (SUBLANES, LANES))

    kinds = widened(types[...])

    def look_up(table):
        return jnp.take_along_axis(widened(table[...]), kinds, axis=1, mode="promise_in_bounds")[0:1, :owned]

    per = LANES // owned
    column = lax.axis_index("col")
    forward = jnp.bitwise_and(marks[...], (1 << BAND) - 1).astype(jnp.float32)
    line = lax.broadcasted_iota(jnp.int32, forward.shape, 0)
    picked = jnp.sum(jnp.where(line == lax.div(column, per), forward, 0.0), axis=0, keepdims=True)
    shift = lax.rem(LANES - lax.rem(column, per) * owned, LANES)
    picked = pltpu.roll(jnp.broadcast_to(picked, (SUBLANES, LANES)), shift, 1)[0:1, :owned]

    def everywhere(row):
        return jnp.broadcast_to(row, (replicas, owned))

    second = [everywhere(look_up(radius)), everywhere(look_up(volume)), everywhere(picked)]
    second.append(jnp.zeros((replicas, owned), jnp.float32))
    out_ref[pl.ds(1, replicas, stride=2), :] = jnp.concatenate(second, axis=1)
    charge = everywhere(charges[...])
    moves[0].wait()
    first = [positions[0], positions[1], positions[2], charge]
    out_ref[pl.ds(0, replicas, stride=2), :] = jnp.concatenate(first, axis=1)


def pack(positions, charges, atom_types, exclusions, type_radius, type_volume):
    replicas, _, owned = positions.shape
    lines = exclusions.shape[0] // LANES
    anywhere = pl.BlockSpec(memory_space=pl.ANY)
    return pl.pallas_call(
        pack_kernel,
        out_shape=pltpu.VMEM((replicas * 2, LANES), jnp.float32),
        in_specs=[anywhere] * 6,
        out_specs=pl.BlockSpec(memory_space=pltpu.VMEM),
        scratch_shapes=[
            pltpu.VMEM((3, replicas, owned), jnp.float32),
            pltpu.VMEM((1, owned), jnp.float32),
            pltpu.VMEM((1, owned), jnp.int32),
            pltpu.VMEM((lines, LANES), jnp.int32),
            pltpu.VMEM((1,) + type_radius.shape, jnp.float32),
            pltpu.VMEM((1,) + type_volume.shape, jnp.float32),
            pltpu.SemaphoreType.DMA((6,)),
        ],
        compiler_params=pltpu.CompilerParams(vmem_limit_bytes=4 * 1024 * 1024),
    )(
        *[
            pltpu.with_memory_space_constraint(operand, pltpu.HBM)
            for operand in (
                positions.transpose(1, 0, 2),
                charges[None],
                atom_types[None],
                exclusions.reshape(lines, LANES),
                type_radius[None],
                type_volume[None],
            )
        ]
    )


def conformation_kernel(recv_ref, out_ref, turned, moved, backs, pair_a, pair_b, pair_c, pair_d):
    owners = out_ref.shape[0]
    per = owners // SUBLANES
    owned = LANES // per
    shape = (SUBLANES, LANES)
    half = SUBLANES // 2
    place = lax.axis_index("col")

    def seen(ref, n):
        return ref.at[pl.ds(lax.shift_right_logical(place, 16 + n), ref.shape[0])]

    def dense(k):
        part, first = k // per, k % per * owned
        rows = [recv_ref[pl.ds(2 * j + part, SUBLANES, stride=2 * per), :] for j in range(per)]
        return jnp.concatenate([row[:, first : first + owned] for row in rows], axis=1)

    def keep(k, value, move=None):
        for drop in range(SUBLANES):
            turned[k, drop] = pltpu.roll(value, drop, 0) if drop else value
        moved[k, 0] = value if move is None else move

    x, y, z, q, rho, vol, marks = [dense(k) for k in range(7)]
    for k, value in ((X, x), (Y, y), (Z, z), (RHO2, rho * rho), (VOL, vol)):
        keep(k, value)
    zero = jnp.zeros(shape, jnp.float32)
    one = jnp.ones(shape, jnp.float32)

    def sweep(pair, names, fields):
        total = [[zero] * 4 for _ in range(fields)]
        edges = (0, TURNS)
        moved_later, backs_later = seen(moved, 0), seen(backs, 0)
        for part in range(2):
            drops = list(range(part * half, (part + 1) * half))
            stay = {drop: [zero] * fields for drop in drops}
            for turn in range(TURNS + 1):
                if turn == 0:
                    mover = {k: moved[k, 0] for k in names}
                elif part == 0:
                    mover = {k: pltpu.roll(moved[k, 0], turn, 1) for k in names}
                    for k in names:
                        moved[k, turn] = mover[k]
                else:
                    mover = {k: moved_later[k, turn] for k in names}
                back = None
                for drop in drops:
                    if turn in edges and drop > half:
                        continue
                    stayer = {k: turned[k, drop] for k in names}
                    to_mover, to_stayer = pair(mover, stayer, turn, drop)
                    stay[drop] = [a + b for a, b in zip(stay[drop], to_stayer)]
                    if turn in edges and drop in (0, half):
                        continue
                    back = to_mover if back is None else [a + b for a, b in zip(back, to_mover)]
                if part == 0 and turn not in edges:
                    for k in range(fields):
                        backs[k, turn] = back[k]
                elif back is not None:
                    for k in range(fields):
                        value = back[k] if turn in edges else back[k] + backs_later[k, turn]
                        value = pltpu.roll(value, LANES - turn, 1) if turn else value
                        total[k][turn % 4] = total[k][turn % 4] + value
            for n, drop in enumerate(drops):
                for k in range(fields):
                    value = pltpu.roll(stay[drop][k], SUBLANES - drop, 0) if drop else stay[drop][k]
                    total[k][n] = total[k][n] + value
        return [(t[0] + t[1]) + (t[2] + t[3]) for t in total]

    def itself(turn, drop):
        return turn == 0 and drop == 0

    def descreen(mover, stayer, turn, drop):
        dx, dy, dz = [mover[k] - stayer[k] for k in (X, Y, Z)]
        distsq = dx * dx + dy * dy + dz * dz
        inv_mover = pltpu.reciprocal(distsq + mover[RHO2], approx=True)
        inv_stayer = pltpu.reciprocal(distsq + stayer[RHO2], approx=True)
        from_mover = mover[VOL] * (inv_mover * inv_mover)
        from_stayer = stayer[VOL] * (inv_stayer * inv_stayer)
        pair_a[turn, drop] = distsq
        pair_b[turn, drop] = from_mover * inv_mover
        pair_c[turn, drop] = from_stayer * inv_stayer
        if itself(turn, drop):
            return [zero], [zero]
        return [from_stayer], [from_mover]

    (integral,) = sweep(descreen, (X, Y, Z, RHO2, VOL), 1)
    inv_rho = pltpu.reciprocal(rho, approx=True)
    inv_shell = pltpu.reciprocal(rho + 0.09, approx=True)
    saturation = jnp.tanh(rho * integral)
    inv_born = inv_rho - saturation * inv_shell
    born = pltpu.reciprocal(inv_born, approx=True)
    decay = (math.sqrt(math.log2(math.e)) / 2.0) * inv_born
    keep(BORN, born)
    keep(DECAY, decay, -decay)
    keep(QBORN, q * born)
    slope = born * born * (1.0 - saturation * saturation) * (rho * inv_shell)
    to_chain = (2.0 * SOLVENT_FACTOR * math.log(2.0)) * q * slope
    marks = marks.astype(jnp.int32)
    lane = lax.broadcasted_iota(jnp.int32, shape, 1)

    def hidden(turn, drop):
        marked = jnp.bitwise_and(jnp.right_shift(pltpu.roll(marks, turn, 1), turn - 1), 1) == 1
        return marked & (lane >= turn if drop == 0 else lane < turn)

    distances = seen(pair_a, 3)

    def born_terms(mover, stayer, turn, drop):
        distsq = distances[turn, drop]
        power = distsq * (mover[DECAY] * stayer[DECAY])
        damping = jnp.exp2(power)
        effective = distsq + (mover[BORN] * stayer[BORN]) * damping
        inverse = lax.rsqrt(effective)
        cubed = inverse * inverse * inverse
        pair_d[turn, drop] = cubed * (SOLVENT_FACTOR - (0.25 * SOLVENT_FACTOR) * damping)
        radial = cubed * (damping * (1.0 / math.log(2.0) - power))
        return [radial * stayer[QBORN]], [radial * mover[QBORN]]

    (radial,) = sweep(born_terms, (BORN, DECAY, QBORN), 1)
    keep(CHAIN, radial * to_chain)
    keep(Q, q)

    kept_a, kept_b, kept_c, kept_d = [seen(ref, 4) for ref in (pair_a, pair_b, pair_c, pair_d)]

    def force_terms(mover, stayer, turn, drop):
        if itself(turn, drop):
            return [zero] * 3, [zero] * 3
        chain = stayer[CHAIN] * kept_b[turn, drop] + mover[CHAIN] * kept_c[turn, drop]
        bare = lax.rsqrt(kept_a[turn, drop])
        bare = bare * bare * bare
        if drop in (0, SUBLANES - 1) and 1 <= turn <= BAND:
            bare = jnp.where(hidden(turn, drop), 0.0, bare)
        factor = chain + (bare - kept_d[turn, drop]) * (mover[Q] * stayer[Q])
        push = [factor * (mover[k] - stayer[k]) for k in (X, Y, Z)]
        return push, [-p for p in push]

    results = sweep(force_terms, (X, Y, Z, Q, CHAIN), 3) + [born]
    for j in range(per):
        out_ref[pl.ds(j, SUBLANES, stride=per), :] = jnp.concatenate(
            [value[:, j * owned : (j + 1) * owned] for value in results], axis=1
        )


def whole_conformation(recv):
    vmem = pl.BlockSpec(memory_space=pltpu.VMEM)
    dense = (SUBLANES, LANES)
    kept = pltpu.VMEM((TURNS + 1, SUBLANES) + dense, jnp.float32)
    return pl.pallas_call(
        conformation_kernel,
        out_shape=jax.ShapeDtypeStruct((recv.shape[0] // 2, LANES), jnp.float32),
        in_specs=[vmem],
        out_specs=vmem,
        scratch_shapes=[
            pltpu.VMEM((10, SUBLANES) + dense, jnp.float32),
            pltpu.VMEM((10, TURNS + 1) + dense, jnp.float32),
            pltpu.VMEM((3, TURNS + 1) + dense, jnp.float32),
            kept,
            kept,
            kept,
            kept,
        ],
        compiler_params=pltpu.CompilerParams(vmem_limit_bytes=32 * 1024 * 1024),
    )(recv)


def unpack_kernel(back_ref, forces_any, born_any, forces, born, sent):
    owned = born.shape[1]
    born[...] = back_ref[:, 3 * owned : 4 * owned]
    moves = [pltpu.make_async_copy(born, born_any, sent.at[3])]
    moves[0].start()
    for axis in range(3):
        forces[axis] = back_ref[:, axis * owned : (axis + 1) * owned]
        moves.append(pltpu.make_async_copy(forces.at[axis], forces_any.at[axis], sent.at[axis]))
        moves[-1].start()
    for move in moves:
        move.wait()


def unpack(back):
    replicas, width = back.shape
    owned = width // 4
    forces = ((3, replicas, owned), jnp.float32)
    born = ((replicas, owned), jnp.float32)
    anywhere = pl.BlockSpec(memory_space=pl.ANY)
    forces, born = pl.pallas_call(
        unpack_kernel,
        out_shape=[jax.ShapeDtypeStruct(*forces), jax.ShapeDtypeStruct(*born)],
        in_specs=[pl.BlockSpec(memory_space=pltpu.VMEM)],
        out_specs=[anywhere, anywhere],
        scratch_shapes=[pltpu.VMEM(*forces), pltpu.VMEM(*born), pltpu.SemaphoreType.DMA((4,))],
        compiler_params=pltpu.CompilerParams(vmem_limit_bytes=4 * 1024 * 1024),
    )(pltpu.with_memory_space_constraint(back, pltpu.VMEM))
    return (forces.transpose(1, 0, 2), born)


def shared_sum(kernel, own, everyone, fields):
    conformations, planes, count = everyone.shape
    tiles = count // LANES
    tiled = everyone.reshape(conformations, planes, tiles, LANES).transpose(2, 0, 1, 3)
    ids = jnp.arange(count, dtype=jnp.int32).reshape(tiles, LANES)

    def advance(running, piece):
        return (running + kernel(own, *piece), None)

    start = jnp.zeros((fields, conformations, own[0].shape[2]), jnp.float32)
    return lax.scan(advance, start, (tiled, ids))[0]


def split_pair(own, tile):
    atoms = [own[0][:, k, :, None] for k in range(own[0].shape[1])]
    others = [tile[:, k, None, :] for k in range(tile.shape[1])]
    displace = jnp.stack([atoms[k] - others[k] for k in range(3)])
    return (atoms, others, displace, jnp.sum(displace * displace, axis=0))


def shared_descreen(own, tile, ids):
    atoms, others, displace, distsq = split_pair(own, tile)
    inverse = 1.0 / (distsq + others[4] * others[4])
    terms = jnp.where(own[1][:, None] != ids[None, :], others[5] * inverse * inverse, 0.0)
    return jnp.sum(terms, axis=2)[None]


def shared_born(own, tile, ids):
    atoms, others, displace, distsq = split_pair(own, tile)
    gap = ids[None, :] - own[1][:, None]
    nearby = (gap != 0) & (jnp.abs(gap) <= BAND)
    position = jnp.where(nearby, jnp.where(gap > 0, gap - 1, BAND - 1 - gap), 0)
    marked = jnp.bitwise_and(jnp.right_shift(own[2][:, None], position), 1) == 1
    weight = jnp.where((gap == 0) | (nearby & marked), 0.0, 1.0)
    bare = lax.rsqrt(jnp.where(gap == 0, 1.0, distsq))
    product = atoms[6] * others[6]
    power = distsq / (4.0 * product)
    damping = jnp.exp(-power)
    inverse = lax.rsqrt(distsq + product * damping)
    cubed = SOLVENT_FACTOR * (atoms[3] * others[3]) * inverse * inverse * inverse
    radial = jnp.sum(0.5 * cubed * damping * (1.0 + power) * others[6], axis=2)
    coulomb = weight * (atoms[3] * others[3]) * bare * bare * bare
    factor = cubed * (1.0 - 0.25 * damping) - coulomb
    return jnp.concatenate([radial[None], jnp.sum(factor[None] * displace, axis=3)])


def shared_chain(own, tile, ids):
    atoms, others, displace, distsq = split_pair(own, tile)
    inv_own = 1.0 / (distsq + atoms[4] * atoms[4])
    inv_other = 1.0 / (distsq + others[4] * others[4])
    factor = atoms[6] * others[5] * (inv_other * inv_other * inv_other)
    factor = factor + others[6] * atoms[5] * (inv_own * inv_own * inv_own)
    return jnp.sum(-4.0 * factor[None] * displace, axis=3)


def shared_conformation(type_radius, type_volume, packed, exclusions, axis):
    kinds = packed[:, 4].astype(jnp.int32)
    radius = type_radius[kinds]
    volume = type_volume[kinds]
    base = jnp.concatenate([packed[:, :4], radius[:, None], volume[:, None]], axis=1)
    length = packed.shape[2]
    ids = lax.axis_index(axis) * length + jnp.arange(length, dtype=jnp.int32)

    def gathered(block):
        return lax.all_gather(block, axis, axis=2, tiled=True)

    everyone = gathered(base)
    integral = shared_sum(shared_descreen, (base, ids, exclusions), everyone, 1)[0]
    saturation = jnp.tanh(radius * integral)
    born = 1.0 / (1.0 / radius - saturation / (radius + 0.09))
    slope = born * born * (1.0 - saturation * saturation) * radius / (radius + 0.09)
    with_born = jnp.concatenate([everyone, gathered(born[:, None])], axis=1)
    own_born = jnp.concatenate([base, born[:, None]], axis=1)
    second = shared_sum(shared_born, (own_born, ids, exclusions), with_born, 4)
    chained = second[0] * slope
    with_chain = jnp.concatenate([everyone, gathered(chained[:, None])], axis=1)
    own_chain = jnp.concatenate([base, chained[:, None]], axis=1)
    third = shared_sum(shared_chain, (own_chain, ids, exclusions), with_chain, 3)
    return jnp.concatenate([-(second[1:] + third), born[None]]).transpose(1, 0, 2)


def on_device(positions, charges, atom_types, exclusions, type_radius, type_volume):
    replicas, _, owned = positions.shape
    columns = lax.axis_size("col")
    devices = lax.axis_size("row") * columns
    if replicas == devices and devices * owned == SUBLANES * LANES:
        both = ("row", "col")
        packed = pack(positions, charges, atom_types, exclusions, type_radius, type_volume)
        recv = lax.all_to_all(packed.reshape(replicas, 2, LANES), both, split_axis=0, concat_axis=0, tiled=True)
        result = whole_conformation(recv.reshape(replicas * 2, LANES))
        back = lax.all_to_all(result.reshape(replicas, 1, LANES), both, split_axis=0, concat_axis=0, tiled=True)
        return unpack(back.reshape(replicas, LANES))
    shared = jnp.concatenate([charges, atom_types.astype(jnp.float32)])
    planes = [positions.reshape(replicas, 3 * owned), jnp.broadcast_to(shared[None], (replicas, 2 * owned))]
    local = replicas // columns
    recv = lax.all_to_all(jnp.concatenate(planes, axis=1), "col", split_axis=0, concat_axis=0, tiled=True)
    recv = recv.reshape(columns, local, 5, owned).transpose(1, 2, 0, 3).reshape(local, 5, columns * owned)
    result = shared_conformation(type_radius, type_volume, recv, exclusions, "row")
    result = result.reshape(local, 4, columns, owned).transpose(2, 0, 1, 3).reshape(replicas, 4 * owned)
    back = lax.all_to_all(result, "col", split_axis=0, concat_axis=0, tiled=True).reshape(replicas, 4, owned)
    return (back[:, :3], back[:, 3])


def solution(mesh):
    return jax.shard_map(
        on_device,
        mesh=mesh,
        in_specs=(
            P(None, None, ("row", "col")),
            P(("row", "col")),
            P(("row", "col")),
            P("row"),
            P(),
            P(),
        ),
        out_specs=(P(None, None, ("row", "col")), P(None, ("row", "col"))),
        check_vma=False,
    )
```

```python
from functools import partial
import math

import jax
import jax.numpy as jnp
from jax import lax
from jax.experimental import pallas as pl
from jax.experimental.pallas import tpu as pltpu
from jax.sharding import PartitionSpec as P

SOLVENT_FACTOR = 1.0 - 1.0 / 78.5
LANES = 128
SUBLANES = 8
BAND = 15


TURNS = 64
X, Y, Z, Q, RHO2, VOL, BORN, DECAY, QBORN, CHAIN = range(10)


def pack_kernel(positions_any, charges_any, types_any, marks_any, radius_any, volume_any, out_ref,
                positions, charges, types, marks, radius, volume, arrived):
    moves = []
    for n, (source, target) in enumerate(
        (
            (positions_any, positions),
            (charges_any, charges),
            (types_any, types),
            (marks_any, marks),
            (radius_any, radius),
            (volume_any, volume),
        )
    ):
        moves.append(pltpu.make_async_copy(source, target, arrived.at[n]))
        moves[-1].start()
    for move in moves:
        move.wait()
    replicas, owned = positions.shape[1:]

    def widened(line):
        line = jnp.concatenate([line, jnp.zeros((1, LANES - line.shape[1]), line.dtype)], axis=1)
        return jnp.broadcast_to(line, (SUBLANES, LANES))

    kinds = widened(types[...])

    def look_up(table):
        return jnp.take_along_axis(widened(table[...]), kinds, axis=1, mode="promise_in_bounds")[0:1, :owned]

    per = LANES // owned
    column = lax.axis_index("col")
    forward = jnp.bitwise_and(marks[...], (1 << BAND) - 1).astype(jnp.float32)
    line = lax.broadcasted_iota(jnp.int32, forward.shape, 0)
    picked = jnp.sum(jnp.where(line == lax.div(column, per), forward, 0.0), axis=0, keepdims=True)
    shift = lax.rem(LANES - lax.rem(column, per) * owned, LANES)
    picked = pltpu.roll(jnp.broadcast_to(picked, (SUBLANES, LANES)), shift, 1)[0:1, :owned]

    def everywhere(row):
        return jnp.broadcast_to(row, (replicas, owned))

    first = [positions[0], positions[1], positions[2], everywhere(charges[...])]
    second = [everywhere(look_up(radius)), everywhere(look_up(volume)), everywhere(picked), jnp.zeros((replicas, owned), jnp.float32)]
    out_ref[pl.ds(0, replicas, stride=2), :] = jnp.concatenate(first, axis=1)
    out_ref[pl.ds(1, replicas, stride=2), :] = jnp.concatenate(second, axis=1)


def pack(positions, charges, atom_types, exclusions, type_radius, type_volume):
    replicas, _, owned = positions.shape
    lines = exclusions.shape[0] // LANES
    anywhere = pl.BlockSpec(memory_space=pl.ANY)
    return pl.pallas_call(
        pack_kernel,
        out_shape=pltpu.VMEM((replicas * 2, LANES), jnp.float32),
        in_specs=[anywhere] * 6,
        out_specs=pl.BlockSpec(memory_space=pltpu.VMEM),
        scratch_shapes=[
            pltpu.VMEM((3, replicas, owned), jnp.float32),
            pltpu.VMEM((1, owned), jnp.float32),
            pltpu.VMEM((1, owned), jnp.int32),
            pltpu.VMEM((lines, LANES), jnp.int32),
            pltpu.VMEM((1,) + type_radius.shape, jnp.float32),
            pltpu.VMEM((1,) + type_volume.shape, jnp.float32),
            pltpu.SemaphoreType.DMA((6,)),
        ],
        compiler_params=pltpu.CompilerParams(vmem_limit_bytes=4 * 1024 * 1024),
    )(
        *[
            pltpu.with_memory_space_constraint(operand, pltpu.HBM)
            for operand in (
                positions.transpose(1, 0, 2),
                charges[None],
                atom_types[None],
                exclusions.reshape(lines, LANES),
                type_radius[None],
                type_volume[None],
            )
        ]
    )


def conformation_kernel(recv_ref, out_ref, turned, moved, backs, pair_a, pair_b, pair_c, pair_d, pair_e):
    owners = out_ref.shape[0]
    per = owners // SUBLANES
    owned = LANES // per
    shape = (SUBLANES, LANES)
    half = SUBLANES // 2
    place = lax.axis_index("col")

    def seen(ref, n):
        return ref.at[pl.ds(lax.shift_right_logical(place, 16 + n), ref.shape[0])]

    def dense(k):
        part, first = k // per, k % per * owned
        rows = [recv_ref[pl.ds(2 * j + part, SUBLANES, stride=2 * per), :] for j in range(per)]
        return jnp.concatenate([row[:, first : first + owned] for row in rows], axis=1)

    def keep(k, value, move=None):
        for drop in range(SUBLANES):
            turned[k, drop] = pltpu.roll(value, drop, 0) if drop else value
        moved[k, 0] = value if move is None else move

    x, y, z, q, rho, vol, marks = [dense(k) for k in range(7)]
    for k, value in ((X, x), (Y, y), (Z, z), (RHO2, rho * rho), (VOL, vol)):
        keep(k, value)
    zero = jnp.zeros(shape, jnp.float32)
    one = jnp.ones(shape, jnp.float32)

    def sweep(pair, names, fields):
        total = [[zero] * 4 for _ in range(fields)]
        edges = (0, TURNS)
        moved_later, backs_later = seen(moved, 0), seen(backs, 0)
        for part in range(2):
            drops = list(range(part * half, (part + 1) * half))
            stay = {drop: [zero] * fields for drop in drops}
            for turn in range(TURNS + 1):
                if turn == 0:
                    mover = {k: moved[k, 0] for k in names}
                elif part == 0:
                    mover = {k: pltpu.roll(moved[k, 0], turn, 1) for k in names}
                    for k in names:
                        moved[k, turn] = mover[k]
                else:
                    mover = {k: moved_later[k, turn] for k in names}
                back = None
                here = seen(turned, turn % 13)
                for drop in drops:
                    if turn in edges and drop > half:
                        continue
                    stayer = {k: here[k, drop] for k in names}
                    to_mover, to_stayer = pair(mover, stayer, turn, drop)
                    stay[drop] = [a + b for a, b in zip(stay[drop], to_stayer)]
                    if turn in edges and drop in (0, half):
                        continue
                    back = to_mover if back is None else [a + b for a, b in zip(back, to_mover)]
                if part == 0 and turn not in edges:
                    for k in range(fields):
                        backs[k, turn] = back[k]
                elif back is not None:
                    for k in range(fields):
                        value = back[k] if turn in edges else back[k] + backs_later[k, turn]
                        value = pltpu.roll(value, LANES - turn, 1) if turn else value
                        total[k][turn % 4] = total[k][turn % 4] + value
            for n, drop in enumerate(drops):
                for k in range(fields):
                    value = pltpu.roll(stay[drop][k], SUBLANES - drop, 0) if drop else stay[drop][k]
                    total[k][n] = total[k][n] + value
        return [(t[0] + t[1]) + (t[2] + t[3]) for t in total]

    def itself(turn, drop):
        return turn == 0 and drop == 0

    def descreen(mover, stayer, turn, drop):
        dx, dy, dz = [mover[k] - stayer[k] for k in (X, Y, Z)]
        distsq = dx * dx + dy * dy + dz * dz
        inv_mover = pltpu.reciprocal(distsq + mover[RHO2], approx=True)
        inv_stayer = pltpu.reciprocal(distsq + stayer[RHO2], approx=True)
        from_mover = mover[VOL] * (inv_mover * inv_mover)
        from_stayer = stayer[VOL] * (inv_stayer * inv_stayer)
        pair_a[turn, drop] = distsq
        pair_b[turn, drop] = from_mover * inv_mover
        pair_c[turn, drop] = from_stayer * inv_stayer
        if itself(turn, drop):
            return [zero], [zero]
        return [from_stayer], [from_mover]

    (integral,) = sweep(descreen, (X, Y, Z, RHO2, VOL), 1)
    inv_rho = pltpu.reciprocal(rho, approx=True)
    inv_shell = pltpu.reciprocal(rho + 0.09, approx=True)
    saturation = jnp.tanh(rho * integral)
    inv_born = inv_rho - saturation * inv_shell
    born = pltpu.reciprocal(inv_born, approx=True)
    decay = (math.sqrt(math.log2(math.e)) / 2.0) * inv_born
    keep(BORN, born)
    keep(DECAY, decay, -decay)
    keep(QBORN, q * born)
    slope = born * born * (1.0 - saturation * saturation) * (rho * inv_shell)
    to_chain = (2.0 * SOLVENT_FACTOR * math.log(2.0)) * q * slope
    marks = marks.astype(jnp.int32)
    lane = lax.broadcasted_iota(jnp.int32, shape, 1)

    def bare_coulomb(part):
        distances = seen(pair_a, 1 + part)
        for turn in range(TURNS + 1):
            if 1 <= turn <= BAND:
                marked = jnp.bitwise_and(jnp.right_shift(pltpu.roll(marks, turn, 1), turn - 1), 1) == 1
            for drop in range(part * half, (part + 1) * half):
                if itself(turn, drop) or (turn in (0, TURNS) and drop > half):
                    continue
                bare = lax.rsqrt(distances[turn, drop])
                bare = bare * bare * bare
                if 1 <= turn <= BAND and drop in (0, SUBLANES - 1):
                    bare = jnp.where(marked & (lane >= turn if drop == 0 else lane < turn), 0.0, bare)
                pair_e[turn, drop] = bare

    bare_coulomb(0)

    distances = seen(pair_a, 3)

    def born_terms(mover, stayer, turn, drop):
        distsq = distances[turn, drop]
        power = distsq * (mover[DECAY] * stayer[DECAY])
        damping = jnp.exp2(power)
        effective = distsq + (mover[BORN] * stayer[BORN]) * damping
        inverse = lax.rsqrt(effective)
        cubed = inverse * inverse * inverse
        pair_d[turn, drop] = cubed * (SOLVENT_FACTOR - (0.25 * SOLVENT_FACTOR) * damping)
        radial = cubed * (damping * (1.0 / math.log(2.0) - power))
        return [radial * stayer[QBORN]], [radial * mover[QBORN]]

    (radial,) = sweep(born_terms, (BORN, DECAY, QBORN), 1)
    keep(CHAIN, radial * to_chain)
    keep(Q, q)
    bare_coulomb(1)

    kept_b, kept_c, kept_d, kept_e = [seen(ref, 4) for ref in (pair_b, pair_c, pair_d, pair_e)]

    def force_terms(mover, stayer, turn, drop):
        if itself(turn, drop):
            return [zero] * 3, [zero] * 3
        chain = stayer[CHAIN] * kept_b[turn, drop] + mover[CHAIN] * kept_c[turn, drop]
        factor = chain + (kept_e[turn, drop] - kept_d[turn, drop]) * (mover[Q] * stayer[Q])
        push = [factor * (mover[k] - stayer[k]) for k in (X, Y, Z)]
        return push, [-p for p in push]

    results = sweep(force_terms, (X, Y, Z, Q, CHAIN), 3) + [born]
    for j in range(per):
        out_ref[pl.ds(j, SUBLANES, stride=per), :] = jnp.concatenate(
            [value[:, j * owned : (j + 1) * owned] for value in results], axis=1
        )


def whole_conformation(recv):
    vmem = pl.BlockSpec(memory_space=pltpu.VMEM)
    dense = (SUBLANES, LANES)
    kept = pltpu.VMEM((TURNS + 1, SUBLANES) + dense, jnp.float32)
    return pl.pallas_call(
        conformation_kernel,
        out_shape=jax.ShapeDtypeStruct((recv.shape[0] // 2, LANES), jnp.float32),
        in_specs=[vmem],
        out_specs=vmem,
        scratch_shapes=[
            pltpu.VMEM((10, SUBLANES) + dense, jnp.float32),
            pltpu.VMEM((10, TURNS + 1) + dense, jnp.float32),
            pltpu.VMEM((3, TURNS + 1) + dense, jnp.float32),
            kept,
            kept,
            kept,
            kept,
            kept,
        ],
        compiler_params=pltpu.CompilerParams(vmem_limit_bytes=32 * 1024 * 1024),
    )(recv)


def unpack_kernel(back_ref, forces_any, born_any, forces, born, sent):
    owned = born.shape[1]
    born[...] = back_ref[:, 3 * owned : 4 * owned]
    moves = [pltpu.make_async_copy(born, born_any, sent.at[3])]
    moves[0].start()
    for axis in range(3):
        forces[axis] = back_ref[:, axis * owned : (axis + 1) * owned]
        moves.append(pltpu.make_async_copy(forces.at[axis], forces_any.at[axis], sent.at[axis]))
        moves[-1].start()
    for move in moves:
        move.wait()


def unpack(back):
    replicas, width = back.shape
    owned = width // 4
    forces = ((3, replicas, owned), jnp.float32)
    born = ((replicas, owned), jnp.float32)
    anywhere = pl.BlockSpec(memory_space=pl.ANY)
    forces, born = pl.pallas_call(
        unpack_kernel,
        out_shape=[jax.ShapeDtypeStruct(*forces), jax.ShapeDtypeStruct(*born)],
        in_specs=[pl.BlockSpec(memory_space=pltpu.VMEM)],
        out_specs=[anywhere, anywhere],
        scratch_shapes=[pltpu.VMEM(*forces), pltpu.VMEM(*born), pltpu.SemaphoreType.DMA((4,))],
        compiler_params=pltpu.CompilerParams(vmem_limit_bytes=4 * 1024 * 1024),
    )(pltpu.with_memory_space_constraint(back, pltpu.VMEM))
    return (forces.transpose(1, 0, 2), born)


def shared_sum(kernel, own, everyone, fields):
    conformations, planes, count = everyone.shape
    tiles = count // LANES
    tiled = everyone.reshape(conformations, planes, tiles, LANES).transpose(2, 0, 1, 3)
    ids = jnp.arange(count, dtype=jnp.int32).reshape(tiles, LANES)

    def advance(running, piece):
        return (running + kernel(own, *piece), None)

    start = jnp.zeros((fields, conformations, own[0].shape[2]), jnp.float32)
    return lax.scan(advance, start, (tiled, ids))[0]


def split_pair(own, tile):
    atoms = [own[0][:, k, :, None] for k in range(own[0].shape[1])]
    others = [tile[:, k, None, :] for k in range(tile.shape[1])]
    displace = jnp.stack([atoms[k] - others[k] for k in range(3)])
    return (atoms, others, displace, jnp.sum(displace * displace, axis=0))


def shared_descreen(own, tile, ids):
    atoms, others, displace, distsq = split_pair(own, tile)
    inverse = 1.0 / (distsq + others[4] * others[4])
    terms = jnp.where(own[1][:, None] != ids[None, :], others[5] * inverse * inverse, 0.0)
    return jnp.sum(terms, axis=2)[None]


def shared_born(own, tile, ids):
    atoms, others, displace, distsq = split_pair(own, tile)
    gap = ids[None, :] - own[1][:, None]
    nearby = (gap != 0) & (jnp.abs(gap) <= BAND)
    position = jnp.where(nearby, jnp.where(gap > 0, gap - 1, BAND - 1 - gap), 0)
    marked = jnp.bitwise_and(jnp.right_shift(own[2][:, None], position), 1) == 1
    weight = jnp.where((gap == 0) | (nearby & marked), 0.0, 1.0)
    bare = lax.rsqrt(jnp.where(gap == 0, 1.0, distsq))
    product = atoms[6] * others[6]
    power = distsq / (4.0 * product)
    damping = jnp.exp(-power)
    inverse = lax.rsqrt(distsq + product * damping)
    cubed = SOLVENT_FACTOR * (atoms[3] * others[3]) * inverse * inverse * inverse
    radial = jnp.sum(0.5 * cubed * damping * (1.0 + power) * others[6], axis=2)
    coulomb = weight * (atoms[3] * others[3]) * bare * bare * bare
    factor = cubed * (1.0 - 0.25 * damping) - coulomb
    return jnp.concatenate([radial[None], jnp.sum(factor[None] * displace, axis=3)])


def shared_chain(own, tile, ids):
    atoms, others, displace, distsq = split_pair(own, tile)
    inv_own = 1.0 / (distsq + atoms[4] * atoms[4])
    inv_other = 1.0 / (distsq + others[4] * others[4])
    factor = atoms[6] * others[5] * (inv_other * inv_other * inv_other)
    factor = factor + others[6] * atoms[5] * (inv_own * inv_own * inv_own)
    return jnp.sum(-4.0 * factor[None] * displace, axis=3)


def shared_conformation(type_radius, type_volume, packed, exclusions, axis):
    kinds = packed[:, 4].astype(jnp.int32)
    radius = type_radius[kinds]
    volume = type_volume[kinds]
    base = jnp.concatenate([packed[:, :4], radius[:, None], volume[:, None]], axis=1)
    length = packed.shape[2]
    ids = lax.axis_index(axis) * length + jnp.arange(length, dtype=jnp.int32)

    def gathered(block):
        return lax.all_gather(block, axis, axis=2, tiled=True)

    everyone = gathered(base)
    integral = shared_sum(shared_descreen, (base, ids, exclusions), everyone, 1)[0]
    saturation = jnp.tanh(radius * integral)
    born = 1.0 / (1.0 / radius - saturation / (radius + 0.09))
    slope = born * born * (1.0 - saturation * saturation) * radius / (radius + 0.09)
    with_born = jnp.concatenate([everyone, gathered(born[:, None])], axis=1)
    own_born = jnp.concatenate([base, born[:, None]], axis=1)
    second = shared_sum(shared_born, (own_born, ids, exclusions), with_born, 4)
    chained = second[0] * slope
    with_chain = jnp.concatenate([everyone, gathered(chained[:, None])], axis=1)
    own_chain = jnp.concatenate([base, chained[:, None]], axis=1)
    third = shared_sum(shared_chain, (own_chain, ids, exclusions), with_chain, 3)
    return jnp.concatenate([-(second[1:] + third), born[None]]).transpose(1, 0, 2)


def on_device(positions, charges, atom_types, exclusions, type_radius, type_volume):
    replicas, _, owned = positions.shape
    columns = lax.axis_size("col")
    devices = lax.axis_size("row") * columns
    if replicas == devices and devices * owned == SUBLANES * LANES:
        both = ("row", "col")
        packed = pack(positions, charges, atom_types, exclusions, type_radius, type_volume)
        recv = lax.all_to_all(packed.reshape(replicas, 2, LANES), both, split_axis=0, concat_axis=0, tiled=True)
        result = whole_conformation(recv.reshape(replicas * 2, LANES))
        back = lax.all_to_all(result.reshape(replicas, 1, LANES), both, split_axis=0, concat_axis=0, tiled=True)
        return unpack(back.reshape(replicas, LANES))
    shared = jnp.concatenate([charges, atom_types.astype(jnp.float32)])
    planes = [positions.reshape(replicas, 3 * owned), jnp.broadcast_to(shared[None], (replicas, 2 * owned))]
    local = replicas // columns
    recv = lax.all_to_all(jnp.concatenate(planes, axis=1), "col", split_axis=0, concat_axis=0, tiled=True)
    recv = recv.reshape(columns, local, 5, owned).transpose(1, 2, 0, 3).reshape(local, 5, columns * owned)
    result = shared_conformation(type_radius, type_volume, recv, exclusions, "row")
    result = result.reshape(local, 4, columns, owned).transpose(2, 0, 1, 3).reshape(replicas, 4 * owned)
    back = lax.all_to_all(result, "col", split_axis=0, concat_axis=0, tiled=True).reshape(replicas, 4, owned)
    return (back[:, :3], back[:, 3])


def solution(mesh):
    return jax.shard_map(
        on_device,
        mesh=mesh,
        in_specs=(
            P(None, None, ("row", "col")),
            P(("row", "col")),
            P(("row", "col")),
            P("row"),
            P(),
            P(),
        ),
        out_specs=(P(None, None, ("row", "col")), P(None, ("row", "col"))),
        check_vma=False,
    )
```
